32 devices in a mesh: seq: 16 (over z, x, core), dp: 2 (over y).
Axes of the slice: x: 2, y: 2, z: 4, core: 2. Of those that a mesh axis runs over, the one named last changes fastest.
Arguments:
- inputs: bfloat16 [2, 2048, 768], P('dp', 'seq'), may hold values from -150 to 150
- cotangent: bfloat16 [2, 2048, 768], P('dp', 'seq'), may hold values from -6 to 6
- conv_weight: bfloat16 [768, 768], replicated, may hold values from -0.125 to 0.125
- proj_weight: bfloat16 [256, 768], replicated, may hold values from -0.375 to 0.375
- gain_in: float32 [768], replicated, may hold values from 0.5 to 1.5
- bias_in: float32 [768], replicated, may hold values from -0.5 to 0.5
- gain_mid: float32 [256], replicated, may hold values from 0.5 to 1.5
- bias_mid: float32 [256], replicated, may hold values from -0.5 to 0.5
Outputs:
- block_out: bfloat16 [2, 2048, 768], P('dp', 'seq')
- input_grad: bfloat16 [2, 2048, 768], P('dp', 'seq')
- conv_grad: float32 [768, 768], P('seq')
- proj_grad: float32 [768, 256], P('seq')
The draws below stay inside these ranges and needn't reach their ends.
All inputs are finite; a program needn't handle non-finite values.
Results may differ from the reference program's by a relative error of at most 0.015.
Values may be sent and summed in bfloat16 or wider, within the bound.
A program may use at most 64 MiB of HBM per device.

```python
import math
import jax
import jax.numpy as jnp
from jax import lax

CH = 768
MID = 256
LENGTH = 2048
BATCH = 2
DILATION_RATE = 1024


def draw_inputs(key, part):
    key_base, key_chan = jax.random.split(jax.random.fold_in(key, 17), 2)
    places = jnp.arange(LENGTH, dtype=jnp.float32)
    rising = 1.0 + 2.0 * places / (LENGTH - 1)
    channel_scale = jnp.exp(jax.random.uniform(key_chan, (CH,), jnp.float32, 0.0, math.log(10.0)))
    base = jax.random.truncated_normal(key_base, -4.0, 4.0, (BATCH, LENGTH, CH), jnp.float32)
    return (base * rising[None, :, None] * channel_scale).astype(jnp.bfloat16)


def with_spikes(result, rng, source, target, shards_of, factor):
    owner, partner = [(jnp.arange(result.shape[dim]) // (result.shape[dim] // shards_of)).reshape([-1 if axis == dim else 1 for axis in range(result.ndim)]) for dim in (source, target)]
    chosen = jax.random.permutation(rng, shards_of)[partner]
    strong = (owner == chosen) | (owner == (partner + shards_of // 2) % shards_of)
    return jnp.where(strong, factor * result, result)


def level_of(key, shape, shards, low, top_value):
    factor_of, own = 1.0, jax.random.fold_in(key, 6)
    for dim, parts in shards:
        steps = jnp.exp(jax.random.uniform(jax.random.fold_in(own, dim), (parts,), jnp.float32, low / len(shards), top_value / len(shards)))
        factor_of = factor_of * jnp.repeat(steps, shape[dim] // parts).reshape([-1 if axis == dim else 1 for axis in range(len(shape))])
    return factor_of


def gaussian(stream_key, dims, scale, reach, cuts=(), held_as=jnp.bfloat16):
    factor_of = level_of(stream_key, dims, cuts, -0.22, 0.18) if cuts else 1.0
    drawn = jax.random.normal(stream_key, dims, jnp.float32) * scale * factor_of
    return jnp.minimum(jnp.maximum(drawn, -reach), reach).astype(held_as)


def bell_draw_with(key, extent, scale, reach, cuts, heavy, kind=jnp.bfloat16):
    entries = scale * jax.random.normal(key, extent, jnp.float32)
    if cuts:
        entries = entries * level_of(key, extent, cuts, -0.22, 0.18)
    return jnp.clip(with_spikes(entries, jax.random.fold_in(key, 3), *heavy), -reach, reach).astype(kind)


def setup_inputs(seed: int = 0) -> dict:
    keys = jax.random.split(jax.random.key(seed), 9)
    inputs = draw_inputs(jax.random.fold_in(keys[8], 71), 0)
    cotangent = bell_draw_with(keys[1], (BATCH, LENGTH, CH), 1.0, 6.0, ((0, 2), (1, 16)), (1, 2, 16, 2.0))
    conv_weight = gaussian(keys[2], (CH, 3 * MID), (3 * CH) ** -0.5, 0.125)
    proj_weight = gaussian(keys[3], (MID, CH), MID ** -0.5, 0.375)
    gain_in = jnp.clip(1.0 + 0.1 * jax.random.normal(keys[4], (CH,), jnp.float32), 0.5, 1.5)
    bias_in = jnp.clip(jax.random.uniform(keys[5], (CH,), jnp.float32, -0.5, 0.5), -0.5, 0.5)
    gain_mid = jnp.clip(1.0 + 0.1 * jax.random.normal(keys[6], (MID,), jnp.float32), 0.5, 1.5)
    bias_mid = jnp.clip(jax.random.uniform(keys[7], (MID,), jnp.float32, -0.5, 0.5), -0.5, 0.5)
    return dict(inputs=inputs, cotangent=cotangent, conv_weight=conv_weight, proj_weight=proj_weight, gain_in=gain_in, bias_in=bias_in, gain_mid=gain_mid, bias_mid=bias_mid)


def gelu_tanh(value):
    coeff = math.sqrt(2.0 / math.pi)
    return 0.5 * value * (1.0 + jnp.tanh(coeff * (value + 0.044715 * value * value * value)))

def gelu_slope(value):
    coeff = math.sqrt(2.0 / math.pi)
    inner = jnp.tanh(coeff * (value + 0.044715 * value * value * value))
    return 0.5 * (1.0 + inner) + 0.5 * value * (1.0 - inner * inner) * coeff * (1.0 + 3.0 * 0.044715 * value * value)

def following_window(value, steps):
    return jnp.concatenate([jnp.zeros_like(value[:, :steps]), value[:, :-steps]], axis=1)

def preceding_window(value, steps):
    return jnp.concatenate([value[:, steps:], jnp.zeros_like(value[:, :steps])], axis=1)

def normalize(value):
    center = lax.optimization_barrier(jnp.mean(value, axis=(0, 1)))
    spread = jnp.sqrt(lax.optimization_barrier(jnp.mean((value - center) ** 2, axis=(0, 1))) + 1e-05)
    return ((value - center) / spread, spread)

def back_norm(dpre, normed, gain, spread):
    first = lax.optimization_barrier(jnp.mean(dpre, axis=(0, 1)))
    second = lax.optimization_barrier(jnp.mean(dpre * normed, axis=(0, 1)))
    return gain * (dpre - first - normed * second) / spread

def reference(inputs, cotangent, conv_weight, proj_weight, gain_in, bias_in, gain_mid, bias_mid):
    width = CH
    central_window = MID
    overall_row_count = BATCH * LENGTH
    stream = inputs.astype(jnp.float32)
    normed_in, spread_in = normalize(stream)
    pre_in = gain_in * normed_in + bias_in
    act_in = gelu_tanh(pre_in).astype(jnp.bfloat16)
    flat_in = act_in.reshape(overall_row_count, width)
    summand_terms = jnp.dot(flat_in, conv_weight, preferred_element_type=jnp.float32).reshape(BATCH, LENGTH, 3 * central_window)
    dilated_filter_output = following_window(summand_terms[..., :central_window], DILATION_RATE) + summand_terms[..., central_window:2 * central_window] + preceding_window(summand_terms[..., 2 * central_window:], DILATION_RATE)
    normed_mid, spread_mid = normalize(dilated_filter_output)
    pre_mid = gain_mid * normed_mid + bias_mid
    act_mid = gelu_tanh(pre_mid).astype(jnp.bfloat16)
    flat_mid = act_mid.reshape(overall_row_count, central_window)
    update = jnp.dot(flat_mid, proj_weight, preferred_element_type=jnp.float32).reshape(BATCH, LENGTH, width)
    block_out = (stream + update).astype(jnp.bfloat16)
    flat_cot = cotangent.reshape(overall_row_count, width)
    proj_grad = lax.dot_general(flat_cot, flat_mid, (((0,), (0,)), ((), ())), preferred_element_type=jnp.float32)
    dact_mid = lax.dot_general(flat_cot, proj_weight, (((1,), (1,)), ((), ())), preferred_element_type=jnp.float32)
    dpre_mid = dact_mid.reshape(BATCH, LENGTH, central_window) * gelu_slope(pre_mid)
    filter_output_gradient = back_norm(dpre_mid, normed_mid, gain_mid, spread_mid).astype(jnp.bfloat16)
    stacked_windows = jnp.concatenate([preceding_window(filter_output_gradient, DILATION_RATE), filter_output_gradient, following_window(filter_output_gradient, DILATION_RATE)], axis=2).reshape(overall_row_count, 3 * central_window)
    conv_grad = lax.dot_general(flat_in, stacked_windows, (((0,), (0,)), ((), ())), preferred_element_type=jnp.float32)
    dact_in = lax.dot_general(stacked_windows, conv_weight, (((1,), (1,)), ((), ())), preferred_element_type=jnp.float32)
    dpre_in = dact_in.reshape(BATCH, LENGTH, width) * gelu_slope(pre_in)
    input_grad = (cotangent.astype(jnp.float32) + back_norm(dpre_in, normed_in, gain_in, spread_in)).astype(jnp.bfloat16)
    return (block_out, input_grad, conv_grad, proj_grad)
```

```python
import functools
import math

import jax
import jax.numpy as jnp
from jax import lax
from jax.experimental import pallas as pl
from jax.experimental.pallas import tpu as pltpu
from jax.sharding import PartitionSpec as P

DILATION = 1024
EPS = 1e-05
COEFF = math.sqrt(2.0 / math.pi)
MESH = pl.DeviceIdType.MESH
F32, BF16 = jnp.float32, jnp.bfloat16


def gelu_inner(v):
    return jnp.tanh(COEFF * (v + 0.044715 * v * v * v))


def gelu_slope(v, inner):
    return 0.5 * (1.0 + inner) + 0.5 * v * (1.0 - inner * inner) * COEFF * (
        1.0 + 3.0 * 0.044715 * v * v
    )


def dot(a, b):
    return jnp.dot(a, b, preferred_element_type=F32)


def dot_t(a, b):
    return lax.dot_general(a, b, (((1,), (1,)), ((), ())), preferred_element_type=F32)


def column_sums(a, b):
    return jnp.concatenate(
        [jnp.sum(a, axis=0, keepdims=True), jnp.sum(b, axis=0, keepdims=True)], axis=0
    )


class Plan:
    def __init__(self, n, m, samples, places, width, mid):
        self.n, self.m = n, m
        self.rows, self.width, self.mid = samples * places, width, mid
        self.counted = float(samples * places * n * m)
        steps = DILATION // places
        inner = 2
        while inner * inner < n:
            inner *= 2
        self.inner, self.nz, self.nx = inner, n // inner, inner // 2
        assert steps % inner == 0 and n % inner == 0
        self.hz = steps // inner
        assert 0 < self.hz < self.nz
        self.block = width // n
        self.padded = -(-self.block // 16) * 16
        if inner * m <= 8:
            self.phases = ("plane", "z")
        else:
            self.phases = ("lo", "dp", "z")
        size = {"plane": inner * m, "lo": inner, "dp": m, "z": self.nz}
        self.sizes = [size[p] for p in self.phases]
        self.slots = sum(s - 1 for s in self.sizes)
        q = self.nz * 2 - 1
        self.sems = 4 * self.slots + 4 * q + self.nx * m - 1 + 2


def kernel(
    plan,
    x_ref, cot_ref, cw_ref, pw_ref, gi_ref, bi_ref, gm_ref, bm_ref,
    out_ref, grad_ref, convg_ref, projg_ref,
    src_w, src_m, got_w, got_m,
    act, h1, pre1, inner1, dact2, before, after, ysend, dact1,
    cot_t, act_t, cot_all, act_all, act2_all, dconv_all, part, parts,
    send_sem, recv_sem, local_sem,
):
    n, m, nz, nx, inner = plan.n, plan.m, plan.nz, plan.nx, plan.inner
    rows, mid, width, block, padded = plan.rows, plan.mid, plan.width, plan.block, plan.padded
    me, dp = lax.axis_index("seq"), lax.axis_index("dp")
    z, lo = lax.div(me, inner), lax.rem(me, inner)
    xi, core = lax.div(lo, 2), lax.rem(lo, 2)
    counter = [0]
    pending = []

    def copy_to(src, dst, target):
        k = counter[0]
        counter[0] += 1
        return pltpu.make_async_remote_copy(
            src_ref=src, dst_ref=dst, send_sem=send_sem.at[k], recv_sem=recv_sem.at[k],
            device_id=target, device_id_type=MESH,
        )

    def push(src, dst, target):
        c = copy_to(src, dst, target)
        c.start()
        pending.append(c)
        return c

    def plane_peer(o):
        j = lax.rem(lo * m + dp + o, inner * m)
        return (z * inner + lax.div(j, m), lax.rem(j, m))

    def z_peer(o, c=None):
        c = core if c is None else c
        return (lax.rem(z + o, nz) * inner + xi * 2 + c, dp)

    peers = {
        "plane": plane_peer,
        "lo": lambda o: (z * inner + lax.rem(lo + o, inner), dp),
        "dp": lambda o: (me, lax.rem(dp + o, m)),
        "z": z_peer,
    }
    core_peer = (z * inner + xi * 2 + (1 - core), dp)

    def reduce_start(src, got, which):
        state = dict(src=src, got=got, which=which, phase=0, base=0)
        launch(state)
        return state

    def launch(st):
        ph = st["phase"]
        st["copies"] = [
            push(st["src"].at[st["which"], ph], st["got"].at[st["which"], st["base"] + o - 1],
                 peers[plan.phases[ph]](o))
            for o in range(1, plan.sizes[ph])
        ]

    def collect(st):
        ph = st["phase"]
        total = st["src"][st["which"], ph]
        for i, c in enumerate(st["copies"]):
            c.wait_recv()
            total = total + st["got"][st["which"], st["base"] + i]
        st["base"] += plan.sizes[ph] - 1
        st["phase"] += 1
        return total

    def reduce_step(st):
        total = collect(st)
        st["src"][st["which"], st["phase"]] = total
        launch(st)

    def reduce_mid(st):
        while st["phase"] < len(plan.phases) - 1:
            reduce_step(st)

    def reduce_end(st):
        reduce_mid(st)
        return collect(st) / plan.counted

    barrier = pltpu.get_barrier_semaphore()
    friends = [plane_peer(o) for o in range(1, inner * m)]
    friends += [z_peer(o, c) for o in range(1, nz) for c in (core, 1 - core)]
    for f in friends:
        pl.semaphore_signal(barrier, inc=1, device_id=f, device_id_type=MESH)

    x = x_ref[...].astype(F32)
    src_w[0, 0] = column_sums(x, x * x)
    pl.semaphore_wait(barrier, len(friends))
    red = reduce_start(src_w, got_w, 0)

    def spread_columns(value, staged, gathered):
        turned = value.T
        if padded != block:
            staged[...] = jnp.zeros_like(staged)
        for i in range(n):
            staged[i // inner, (i % inner) // 2, i % 2, :block, :] = turned[
                i * block : (i + 1) * block, :
            ].astype(BF16)
        q = z * 2 + core
        lanes = pl.ds(pl.multiple_of(q * rows, rows), rows)
        copies = []
        for o in range(nz):
            for c in (core, 1 - core):
                if o == 0 and c is core:
                    continue
                copies.append(
                    push(staged.at[lax.rem(z + o, nz), :, c], gathered.at[:, :, lanes], z_peer(o, c))
                )
        return copies, (staged.at[z, :, core], gathered.at[:, :, lanes])

    cot = cot_ref[...]
    dact2[...] = dot_t(cot, pw_ref[...])
    cot_copies, cot_own = spread_columns(cot.astype(F32), cot_t, cot_all)
    own_cot = pltpu.make_async_copy(*cot_own, local_sem.at[0])
    own_cot.start()

    mean = reduce_end(red)
    center = mean[0:1]
    rs1 = 1.0 / jnp.sqrt(mean[1:2] - center * center + EPS)
    h = (x_ref[...].astype(F32) - center) * rs1
    h1[...] = h
    pre = gi_ref[...] * h + bi_ref[...]
    t = gelu_inner(pre)
    pre1[...] = pre
    inner1[...] = t
    act[...] = (0.5 * pre * (1.0 + t)).astype(BF16)

    steps = plan.hz * inner
    up = copy_to(ysend.at[0], before, (lax.rem(me + steps, n), dp))
    down = copy_to(ysend.at[1], after, (lax.rem(me + n - steps, n), dp))
    has_next, has_prev = me < n - steps, me >= steps

    @pl.when(has_next)
    def _():
        ysend[0] = dot(act[...], cw_ref[:, :mid]).astype(BF16)
        up.start()

    @pl.when(has_prev)
    def _():
        ysend[1] = dot(act[...], cw_ref[:, 2 * mid :]).astype(BF16)
        down.start()

    conv = dot(act[...], cw_ref[:, mid : 2 * mid])
    act_copies, act_own = spread_columns(act[...].astype(F32), act_t, act_all)
    own_act = pltpu.make_async_copy(*act_own, local_sem.at[1])
    own_act.start()

    @pl.when(has_prev)
    def _():
        up.wait_recv()

    @pl.when(jnp.logical_not(has_prev))
    def _():
        before[...] = jnp.zeros_like(before)

    @pl.when(has_next)
    def _():
        down.wait_recv()

    @pl.when(jnp.logical_not(has_next))
    def _():
        after[...] = jnp.zeros_like(after)

    conv = conv + before[...].astype(F32) + after[...].astype(F32)
    src_m[0, 0] = column_sums(conv, conv * conv)
    mean = reduce_end(reduce_start(src_m, got_m, 0))
    center = mean[0:1]
    rs2 = 1.0 / jnp.sqrt(mean[1:2] - center * center + EPS)
    h2 = (conv - center) * rs2
    pre2 = gm_ref[...] * h2 + bm_ref[...]
    t2 = gelu_inner(pre2)
    act2 = (0.5 * pre2 * (1.0 + t2)).astype(BF16)
    dpre2 = dact2[...] * gelu_slope(pre2, t2)
    src_m[1, 0] = column_sums(dpre2, dpre2 * h2)
    red = reduce_start(src_m, got_m, 1)

    def place(zz, c):
        return pl.ds(pl.multiple_of((zz * 2 + c) * rows, rows), rows)

    own = place(z, core)

    def gather_start(full):
        order = sorted(range(1, nz), key=lambda o: o not in (plan.hz, nz - plan.hz))
        over_z = {o: push(full.at[own], full.at[own], z_peer(o)) for o in order}
        return over_z, [push(full.at[own], full.at[own], core_peer)]

    def pass_on(full, over_z, across, o):
        over_z[o].wait_recv()
        piece = full.at[place(lax.rem(z + nz - o, nz), core)]
        across.append(push(piece, piece, core_peer))

    act2_all[own, :] = act2
    act2_z, act2_c = gather_start(act2_all)
    out_ref[...] = (x_ref[...].astype(F32) + dot(act2, pw_ref[...])).astype(BF16)
    mean = reduce_end(red)
    dconv = (gm_ref[...] * (dpre2 - mean[0:1] - h2 * mean[1:2]) * rs2).astype(BF16)
    dconv_all[own, :] = dconv
    dconv_z, dconv_c = gather_start(dconv_all)
    dact1[...] = dot_t(dconv, cw_ref[:, mid : 2 * mid])
    slope1 = gelu_slope(pre1[...], inner1[...])
    pre1[...] = slope1
    halo = sorted({plan.hz, nz - plan.hz})
    for o in halo:
        pass_on(dconv_all, dconv_z, dconv_c, o)

    @pl.when(z + plan.hz < nz)
    def _():
        dact1[...] += dot_t(
            dconv_all[place(lax.rem(z + plan.hz, nz), core), :], cw_ref[:, :mid]
        )

    @pl.when(z >= plan.hz)
    def _():
        dact1[...] += dot_t(
            dconv_all[place(lax.rem(z + nz - plan.hz, nz), core), :], cw_ref[:, 2 * mid :]
        )

    dpre1 = dact1[...] * pre1[...]
    dact1[...] = dpre1
    src_w[1, 0] = column_sums(dpre1, dpre1 * h1[...])
    red = reduce_start(src_w, got_w, 1)

    for o in range(1, nz):
        pass_on(act2_all, act2_z, act2_c, o)
    reduce_mid(red)
    for o in range(1, nz):
        if o not in halo:
            pass_on(dconv_all, dconv_z, dconv_c, o)
    own_cot.wait()
    own_act.wait()
    for c in cot_copies + act_copies + act2_c + dconv_c:
        c.wait_recv()

    depth = nz * 2 * rows
    shift = plan.hz * 2 * rows
    for k in range(nx):
        part[k, :, :mid] = dot(
            act_all[k, :, : depth - shift], dconv_all[shift:, :]
        ).astype(BF16)
        part[k, :, mid : 2 * mid] = dot(act_all[k], dconv_all[...]).astype(BF16)
        part[k, :, 2 * mid : 3 * mid] = dot(
            act_all[k, :, shift:], dconv_all[: depth - shift, :]
        ).astype(BF16)
        part[k, :, 3 * mid :] = dot(cot_all[k], act2_all[...]).astype(BF16)
    group = nx * m
    mine = xi * m + dp
    part_copies = []
    for o in range(1, group):
        to = lax.rem(mine + o, group)
        tx, ty = lax.div(to, m), lax.rem(to, m)
        part_copies.append(
            push(part.at[tx], parts.at[mine], (z * inner + tx * 2 + core, ty))
        )
    parts[pl.ds(mine, 1)] = part[pl.ds(xi, 1)]

    mean = reduce_end(red)
    grad_ref[...] = (
        cot_ref[...].astype(F32)
        + gi_ref[...] * (dact1[...] - mean[0:1] - h1[...] * mean[1:2]) * rs1
    ).astype(BF16)

    for c in part_copies:
        c.wait_recv()
    total = parts[0].astype(F32)
    for k in range(1, group):
        total = total + parts[k].astype(F32)
    convg_ref[...] = total[:block, : 3 * mid]
    projg_ref[...] = total[:block, 3 * mid :]

    for c in pending:
        c.wait_send()

    @pl.when(has_next)
    def _():
        up.wait_send()

    @pl.when(has_prev)
    def _():
        down.wait_send()


def per_device(inputs, cotangent, conv_weight, proj_weight, gain_in, bias_in, gain_mid, bias_mid):
    samples, places, width = inputs.shape
    mid = proj_weight.shape[0]
    plan = Plan(
        lax.axis_size("seq"), lax.axis_size("dp"), samples, places, width, mid
    )
    rows, nz, nx, padded = plan.rows, plan.nz, plan.nx, plan.padded
    depth = nz * 2 * rows
    vmem = pl.BlockSpec(memory_space=pltpu.VMEM)
    phases = len(plan.phases)
    block_out, input_grad, conv_grad, proj_grad = pl.pallas_call(
        functools.partial(kernel, plan),
        out_shape=(
            jax.ShapeDtypeStruct((rows, width), BF16),
            jax.ShapeDtypeStruct((rows, width), BF16),
            jax.ShapeDtypeStruct((plan.block, 3 * mid), F32),
            jax.ShapeDtypeStruct((plan.block, mid), F32),
        ),
        in_specs=[vmem] * 8,
        out_specs=(vmem,) * 4,
        scratch_shapes=[
            pltpu.VMEM((2, phases, 2, width), F32),
            pltpu.VMEM((2, phases, 2, mid), F32),
            pltpu.VMEM((2, plan.slots, 2, width), F32),
            pltpu.VMEM((2, plan.slots, 2, mid), F32),
            pltpu.VMEM((rows, width), BF16),
            pltpu.VMEM((rows, width), F32),
            pltpu.VMEM((rows, width), F32),
            pltpu.VMEM((rows, width), F32),
            pltpu.VMEM((rows, mid), F32),
            pltpu.VMEM((rows, mid), BF16),
            pltpu.VMEM((rows, mid), BF16),
            pltpu.VMEM((2, rows, mid), BF16),
            pltpu.VMEM((rows, width), F32),
            pltpu.VMEM((nz, nx, 2, padded, rows), BF16),
            pltpu.VMEM((nz, nx, 2, padded, rows), BF16),
            pltpu.VMEM((nx, padded, depth), BF16),
            pltpu.VMEM((nx, padded, depth), BF16),
            pltpu.VMEM((depth, mid), BF16),
            pltpu.VMEM((depth, mid), BF16),
            pltpu.VMEM((nx, padded, 4 * mid), BF16),
            pltpu.VMEM((nx * plan.m, padded, 4 * mid), BF16),
            pltpu.SemaphoreType.DMA((plan.sems,)),
            pltpu.SemaphoreType.DMA((plan.sems,)),
            pltpu.SemaphoreType.DMA((2,)),
        ],
        compiler_params=pltpu.CompilerParams(
            collective_id=0, has_side_effects=True, vmem_limit_bytes=32 * 1024 * 1024
        ),
    )(
        inputs.reshape(rows, width),
        cotangent.reshape(rows, width),
        conv_weight,
        proj_weight,
        gain_in.reshape(1, width),
        bias_in.reshape(1, width),
        gain_mid.reshape(1, mid),
        bias_mid.reshape(1, mid),
    )
    shape = (samples, places, width)
    return (block_out.reshape(shape), input_grad.reshape(shape), conv_grad, proj_grad)


def solution(mesh):
    in_specs = (P("dp", "seq", None), P("dp", "seq", None), P(), P(), P(), P(), P(), P())
    out_specs = (P("dp", "seq", None), P("dp", "seq", None), P("seq", None), P("seq", None))
    return jax.shard_map(
        per_device, mesh=mesh, in_specs=in_specs, out_specs=out_specs, check_vma=False
    )
```

```python
import functools
import math

import jax
import jax.numpy as jnp
from jax import lax
from jax.experimental import pallas as pl
from jax.experimental.pallas import tpu as pltpu
from jax.sharding import PartitionSpec as P

DILATION = 1024
EPS = 1e-05
COEFF = math.sqrt(2.0 / math.pi)
MESH = pl.DeviceIdType.MESH
F32, BF16 = jnp.float32, jnp.bfloat16


def gelu_inner(v):
    return jnp.tanh(COEFF * (v + 0.044715 * v * v * v))


def gelu_slope(v, inner):
    return 0.5 * (1.0 + inner) + 0.5 * v * (1.0 - inner * inner) * COEFF * (
        1.0 + 3.0 * 0.044715 * v * v
    )


def dot(a, b):
    return jnp.dot(a, b, preferred_element_type=F32)


def dot_t(a, b):
    return lax.dot_general(a, b, (((1,), (1,)), ((), ())), preferred_element_type=F32)


def column_sums(a, b):
    return jnp.concatenate(
        [jnp.sum(a, axis=0, keepdims=True), jnp.sum(b, axis=0, keepdims=True)], axis=0
    )


class Plan:
    def __init__(self, n, m, samples, places, width, mid):
        self.n, self.m = n, m
        self.rows, self.width, self.mid = samples * places, width, mid
        self.counted = float(samples * places * n * m)
        steps = DILATION // places
        inner = 2
        while inner * inner < n:
            inner *= 2
        self.inner, self.nz, self.nx = inner, n // inner, inner // 2
        assert steps % inner == 0 and n % inner == 0
        self.hz = steps // inner
        assert 0 < self.hz < self.nz
        self.block = width // n
        self.padded = -(-self.block // 16) * 16
        if inner * m <= 8:
            self.phases = ("z", "plane")
        else:
            self.phases = ("z", "lo", "dp")
        size = {"plane": inner * m, "lo": inner, "dp": m, "z": self.nz}
        self.sizes = [size[p] for p in self.phases]
        self.slots = sum(s - 1 for s in self.sizes)
        q = self.nz * 2 - 1
        self.sems = 4 * self.slots + 4 * q + 2 * (self.nx * m - 1) + 2


def kernel(
    plan,
    x_hbm, cot_hbm, cw_hbm, pw_hbm, gi_hbm, bi_hbm, gm_hbm, bm_hbm,
    out_hbm, grad_hbm, convg_hbm, projg_hbm,
    x_ref, cot_ref, cw_ref, pw_ref, gi_ref, bi_ref, gm_ref, bm_ref,
    out_ref, grad_ref, convg_ref, projg_ref,
    src_w, src_m, got_w, got_m,
    act, h1, pre1, inner1, dact2, before, after, ysend, dact1,
    cot_t, act_t, cot_all, act_all, act2_all, dconv_all, part, parts,
    send_sem, recv_sem, local_sem,
):
    n, m, nz, nx, inner = plan.n, plan.m, plan.nz, plan.nx, plan.inner
    rows, mid, width, block, padded = plan.rows, plan.mid, plan.width, plan.block, plan.padded
    me, dp = lax.axis_index("seq"), lax.axis_index("dp")
    z, lo = lax.div(me, inner), lax.rem(me, inner)
    xi, core = lax.div(lo, 2), lax.rem(lo, 2)
    loads = [
        pltpu.make_async_copy(a, b, local_sem.at[2 + i])
        for i, (a, b) in enumerate(
            (
                (x_hbm, x_ref), (cot_hbm, cot_ref), (pw_hbm, pw_ref), (gi_hbm, gi_ref),
                (bi_hbm, bi_ref), (cw_hbm, cw_ref), (gm_hbm, gm_ref), (bm_hbm, bm_ref),
            )
        )
    ]
    stores = [
        pltpu.make_async_copy(a, b, local_sem.at[10 + i])
        for i, (a, b) in enumerate(
            (
                (out_ref, out_hbm), (grad_ref, grad_hbm),
                (convg_ref, convg_hbm), (projg_ref, projg_hbm),
            )
        )
    ]
    for c in loads:
        c.start()
    counter = [0]
    pending = []

    def copy_to(src, dst, target):
        k = counter[0]
        counter[0] += 1
        return pltpu.make_async_remote_copy(
            src_ref=src, dst_ref=dst, send_sem=send_sem.at[k], recv_sem=recv_sem.at[k],
            device_id=target, device_id_type=MESH,
        )

    def push(src, dst, target):
        c = copy_to(src, dst, target)
        c.start()
        pending.append(c)
        return c

    def plane_peer(o):
        j = lax.rem(lo * m + dp + o, inner * m)
        return (z * inner + lax.div(j, m), lax.rem(j, m))

    def z_peer(o, c=None):
        c = core if c is None else c
        return (lax.rem(z + o, nz) * inner + xi * 2 + c, dp)

    peers = {
        "plane": plane_peer,
        "lo": lambda o: (z * inner + lax.rem(lo + o, inner), dp),
        "dp": lambda o: (me, lax.rem(dp + o, m)),
        "z": z_peer,
    }
    core_peer = (z * inner + xi * 2 + (1 - core), dp)

    def reduce_start(src, got, which):
        state = dict(src=src, got=got, which=which, phase=0, base=0)
        launch(state)
        return state

    def launch(st):
        ph = st["phase"]
        st["copies"] = [
            push(st["src"].at[st["which"], ph], st["got"].at[st["which"], st["base"] + o - 1],
                 peers[plan.phases[ph]](o))
            for o in range(1, plan.sizes[ph])
        ]

    def collect(st):
        ph = st["phase"]
        total = st["src"][st["which"], ph]
        for i, c in enumerate(st["copies"]):
            c.wait_recv()
            total = total + st["got"][st["which"], st["base"] + i]
        st["base"] += plan.sizes[ph] - 1
        st["phase"] += 1
        return total

    def reduce_step(st):
        total = collect(st)
        st["src"][st["which"], st["phase"]] = total
        launch(st)

    def reduce_mid(st):
        while st["phase"] < len(plan.phases) - 1:
            reduce_step(st)

    def reduce_end(st):
        reduce_mid(st)
        return collect(st) / plan.counted

    barrier = pltpu.get_barrier_semaphore()
    friends = [plane_peer(o) for o in range(1, inner * m)]
    friends += [z_peer(o, c) for o in range(1, nz) for c in (core, 1 - core)]
    for f in friends:
        pl.semaphore_signal(barrier, inc=1, device_id=f, device_id_type=MESH)

    loads[0].wait()
    x = x_ref[...].astype(F32)
    src_w[0, 0] = column_sums(x, x * x)
    pl.semaphore_wait(barrier, len(friends))
    red = reduce_start(src_w, got_w, 0)

    def stage_columns(value, staged):
        turned = value.T
        if padded != block:
            staged[...] = jnp.zeros_like(staged)
        for i in range(n):
            staged[i // inner, (i % inner) // 2, i % 2, :block, :] = turned[
                i * block : (i + 1) * block, :
            ].astype(BF16)

    def spread_columns(staged, gathered, sem):
        q = z * 2 + core
        lanes = pl.ds(pl.multiple_of(q * rows, rows), rows)
        own = pltpu.make_async_copy(staged.at[z, :, core], gathered.at[:, :, lanes], sem)
        own.start()
        copies = []
        for o in range(nz):
            for c in (core, 1 - core):
                if o == 0 and c is core:
                    continue
                copies.append(
                    push(staged.at[lax.rem(z + o, nz), :, c], gathered.at[:, :, lanes], z_peer(o, c))
                )
        return copies, own

    loads[1].wait()
    loads[2].wait()
    cot = cot_ref[...]
    stage_columns(cot.astype(F32), cot_t)
    reduce_step(red)
    cot_copies, own_cot = spread_columns(cot_t, cot_all, local_sem.at[0])
    dact2[...] = dot_t(cot_ref[...], pw_ref[...])
    for c in loads[3:]:
        c.wait()

    mean = reduce_end(red)
    center = mean[0:1]
    rs1 = 1.0 / jnp.sqrt(mean[1:2] - center * center + EPS)
    h = (x_ref[...].astype(F32) - center) * rs1
    h1[...] = h
    pre = gi_ref[...].reshape(1, -1) * h + bi_ref[...].reshape(1, -1)
    t = gelu_inner(pre)
    pre1[...] = pre
    inner1[...] = t
    act[...] = (0.5 * pre * (1.0 + t)).astype(BF16)

    steps = plan.hz * inner
    up = copy_to(ysend.at[0], before, (lax.rem(me + steps, n), dp))
    down = copy_to(ysend.at[1], after, (lax.rem(me + n - steps, n), dp))
    has_next, has_prev = me < n - steps, me >= steps

    @pl.when(has_next)
    def _():
        ysend[0] = dot(act[...], cw_ref[:, :mid]).astype(BF16)
        up.start()

    @pl.when(has_prev)
    def _():
        ysend[1] = dot(act[...], cw_ref[:, 2 * mid :]).astype(BF16)
        down.start()

    conv = dot(act[...], cw_ref[:, mid : 2 * mid])
    stage_columns(act[...].astype(F32), act_t)

    @pl.when(has_prev)
    def _():
        up.wait_recv()

    @pl.when(jnp.logical_not(has_prev))
    def _():
        before[...] = jnp.zeros_like(before)

    @pl.when(has_next)
    def _():
        down.wait_recv()

    @pl.when(jnp.logical_not(has_next))
    def _():
        after[...] = jnp.zeros_like(after)

    conv = conv + before[...].astype(F32) + after[...].astype(F32)
    src_m[0, 0] = column_sums(conv, conv * conv)
    red = reduce_start(src_m, got_m, 0)
    pre1[...] = gelu_slope(pre1[...], inner1[...])
    reduce_step(red)
    act_copies, own_act = spread_columns(act_t, act_all, local_sem.at[1])
    mean = reduce_end(red)
    center = mean[0:1]
    rs2 = 1.0 / jnp.sqrt(mean[1:2] - center * center + EPS)
    h2 = (conv - center) * rs2
    pre2 = gm_ref[...].reshape(1, -1) * h2 + bm_ref[...].reshape(1, -1)
    t2 = gelu_inner(pre2)
    act2 = (0.5 * pre2 * (1.0 + t2)).astype(BF16)
    dpre2 = dact2[...] * gelu_slope(pre2, t2)
    src_m[1, 0] = column_sums(dpre2, dpre2 * h2)
    red = reduce_start(src_m, got_m, 1)

    def place(zz, c):
        return pl.ds(pl.multiple_of((zz * 2 + c) * rows, rows), rows)

    own = place(z, core)

    def gather_start(full):
        order = sorted(range(1, nz), key=lambda o: o not in (plan.hz, nz - plan.hz))
        over_z = {o: push(full.at[own], full.at[own], z_peer(o)) for o in order}
        return over_z, [push(full.at[own], full.at[own], core_peer)]

    def pass_on(full, over_z, across, o):
        over_z[o].wait_recv()
        piece = full.at[place(lax.rem(z + nz - o, nz), core)]
        across.append(push(piece, piece, core_peer))

    act2_all[own, :] = act2
    reduce_step(red)
    act2_z, act2_c = gather_start(act2_all)
    out_ref[...] = (x_ref[...].astype(F32) + dot(act2, pw_ref[...])).astype(BF16)
    stores[0].start()
    mean = reduce_end(red)
    dconv = (gm_ref[...].reshape(1, -1) * (dpre2 - mean[0:1] - h2 * mean[1:2]) * rs2).astype(BF16)
    dconv_all[own, :] = dconv
    dconv_z, dconv_c = gather_start(dconv_all)
    dact1[...] = dot_t(dconv, cw_ref[:, mid : 2 * mid])
    for o in range(1, nz):
        pass_on(act2_all, act2_z, act2_c, o)
    halo = sorted({plan.hz, nz - plan.hz})
    for o in halo:
        pass_on(dconv_all, dconv_z, dconv_c, o)

    @pl.when(z + plan.hz < nz)
    def _():
        dact1[...] += dot_t(
            dconv_all[place(lax.rem(z + plan.hz, nz), core), :], cw_ref[:, :mid]
        )

    @pl.when(z >= plan.hz)
    def _():
        dact1[...] += dot_t(
            dconv_all[place(lax.rem(z + nz - plan.hz, nz), core), :], cw_ref[:, 2 * mid :]
        )

    dpre1 = dact1[...] * pre1[...]
    dact1[...] = dpre1
    src_w[1, 0] = column_sums(dpre1, dpre1 * h1[...])
    red = reduce_start(src_w, got_w, 1)

    group = nx * m
    mine = xi * m + dp

    def send_parts(columns):
        copies = []
        for o in range(1, group):
            to = lax.rem(mine + o, group)
            tx, ty = lax.div(to, m), lax.rem(to, m)
            copies.append(
                push(
                    part.at[tx, :, columns],
                    parts.at[mine, :, columns],
                    (z * inner + tx * 2 + core, ty),
                )
            )
        parts[pl.ds(mine, 1), :, columns] = part[pl.ds(xi, 1), :, columns]
        return copies

    own_cot.wait()
    for c in cot_copies + act2_c:
        c.wait_recv()
    for k in range(nx):
        part[k, :, 3 * mid :] = dot(cot_all[k], act2_all[...]).astype(BF16)
    reduce_mid(red)
    part_copies = send_parts(pl.ds(3 * mid, mid))
    for o in range(1, nz):
        if o not in halo:
            pass_on(dconv_all, dconv_z, dconv_c, o)
    own_act.wait()
    for c in act_copies + dconv_c:
        c.wait_recv()

    depth = nz * 2 * rows
    shift = plan.hz * 2 * rows
    for k in range(nx):
        part[k, :, :mid] = dot(
            act_all[k, :, : depth - shift], dconv_all[shift:, :]
        ).astype(BF16)
        part[k, :, mid : 2 * mid] = dot(act_all[k], dconv_all[...]).astype(BF16)
        part[k, :, 2 * mid : 3 * mid] = dot(
            act_all[k, :, shift:], dconv_all[: depth - shift, :]
        ).astype(BF16)
    part_copies += send_parts(pl.ds(0, 3 * mid))

    mean = reduce_end(red)
    grad_ref[...] = (
        cot_ref[...].astype(F32)
        + gi_ref[...].reshape(1, -1) * (dact1[...] - mean[0:1] - h1[...] * mean[1:2]) * rs1
    ).astype(BF16)
    stores[1].start()

    for c in part_copies:
        c.wait_recv()
    total = parts[0].astype(F32)
    for k in range(1, group):
        total = total + parts[k].astype(F32)
    convg_ref[...] = total[:block, : 3 * mid]
    projg_ref[...] = total[:block, 3 * mid :]
    stores[2].start()
    stores[3].start()
    for c in stores:
        c.wait()

    for c in pending:
        c.wait_send()

    @pl.when(has_next)
    def _():
        up.wait_send()

    @pl.when(has_prev)
    def _():
        down.wait_send()


def copy_kernel(count, *refs):
    sem = refs[-1]
    copies = [
        pltpu.make_async_copy(refs[i], refs[count + i], sem.at[i]) for i in range(count)
    ]
    for c in copies:
        c.start()
    for c in copies:
        c.wait()


def per_device(inputs, cotangent, conv_weight, proj_weight, gain_in, bias_in, gain_mid, bias_mid):
    samples, places, width = inputs.shape
    mid = proj_weight.shape[0]
    plan = Plan(
        lax.axis_size("seq"), lax.axis_size("dp"), samples, places, width, mid
    )
    rows, nz, nx, padded = plan.rows, plan.nz, plan.nx, plan.padded
    depth = nz * 2 * rows
    hbm = pl.BlockSpec(memory_space=pl.ANY)
    outs = (
        jax.ShapeDtypeStruct((rows, width), BF16),
        jax.ShapeDtypeStruct((rows, width), BF16),
        jax.ShapeDtypeStruct((plan.block, 3 * mid), F32),
        jax.ShapeDtypeStruct((plan.block, mid), F32),
    )
    phases = len(plan.phases)
    results = pl.pallas_call(
        functools.partial(kernel, plan),
        out_shape=outs,
        in_specs=[hbm] * 8,
        out_specs=(hbm,) * 4,
        scratch_shapes=[
            pltpu.VMEM((rows, width), BF16),
            pltpu.VMEM((rows, width), BF16),
            pltpu.VMEM((width, 3 * mid), BF16),
            pltpu.VMEM((mid, width), BF16),
            pltpu.VMEM((width,), F32),
            pltpu.VMEM((width,), F32),
            pltpu.VMEM((mid,), F32),
            pltpu.VMEM((mid,), F32),
            *[pltpu.VMEM(o.shape, o.dtype) for o in outs],
            pltpu.VMEM((2, phases, 2, width), F32),
            pltpu.VMEM((2, phases, 2, mid), F32),
            pltpu.VMEM((2, plan.slots, 2, width), F32),
            pltpu.VMEM((2, plan.slots, 2, mid), F32),
            pltpu.VMEM((rows, width), BF16),
            pltpu.VMEM((rows, width), F32),
            pltpu.VMEM((rows, width), F32),
            pltpu.VMEM((rows, width), F32),
            pltpu.VMEM((rows, mid), F32),
            pltpu.VMEM((rows, mid), BF16),
            pltpu.VMEM((rows, mid), BF16),
            pltpu.VMEM((2, rows, mid), BF16),
            pltpu.VMEM((rows, width), F32),
            pltpu.VMEM((nz, nx, 2, padded, rows), BF16),
            pltpu.VMEM((nz, nx, 2, padded, rows), BF16),
            pltpu.VMEM((nx, padded, depth), BF16),
            pltpu.VMEM((nx, padded, depth), BF16),
            pltpu.VMEM((depth, mid), BF16),
            pltpu.VMEM((depth, mid), BF16),
            pltpu.VMEM((nx, padded, 4 * mid), BF16),
            pltpu.VMEM((nx * plan.m, padded, 4 * mid), BF16),
            pltpu.SemaphoreType.DMA((plan.sems,)),
            pltpu.SemaphoreType.DMA((plan.sems,)),
            pltpu.SemaphoreType.DMA((14,)),
        ],
        compiler_params=pltpu.CompilerParams(
            collective_id=0, has_side_effects=True, vmem_limit_bytes=56 * 1024 * 1024
        ),
    )(
        inputs.reshape(rows, width),
        cotangent.reshape(rows, width),
        conv_weight,
        proj_weight,
        gain_in,
        bias_in,
        gain_mid,
        bias_mid,
    )
    block_out, input_grad, conv_grad, proj_grad = pl.pallas_call(
        functools.partial(copy_kernel, len(outs)),
        out_shape=outs,
        in_specs=[hbm] * len(outs),
        out_specs=(hbm,) * len(outs),
        scratch_shapes=[pltpu.SemaphoreType.DMA((len(outs),))],
        compiler_params=pltpu.CompilerParams(vmem_limit_bytes=56 * 1024 * 1024),
    )(*results)
    shape = (samples, places, width)
    return (block_out.reshape(shape), input_grad.reshape(shape), conv_grad, proj_grad)


def solution(mesh):
    in_specs = (P("dp", "seq", None), P("dp", "seq", None), P(), P(), P(), P(), P(), P())
    out_specs = (P("dp", "seq", None), P("dp", "seq", None), P("seq", None), P("seq", None))
    return jax.shard_map(
        per_device, mesh=mesh, in_specs=in_specs, out_specs=out_specs, check_vma=False
    )
```

```python
import functools
import math

import jax
import jax.numpy as jnp
from jax import lax
from jax.experimental import pallas as pl
from jax.experimental.pallas import tpu as pltpu
from jax.sharding import PartitionSpec as P

DILATION = 1024
EPS = 1e-05
COEFF = math.sqrt(2.0 / math.pi)
MESH = pl.DeviceIdType.MESH
F32, BF16 = jnp.float32, jnp.bfloat16


def gelu_inner(v):
    return jnp.tanh(COEFF * (v + 0.044715 * v * v * v))


def gelu_slope(v, inner):
    return 0.5 * (1.0 + inner) + 0.5 * v * (1.0 - inner * inner) * COEFF * (
        1.0 + 3.0 * 0.044715 * v * v
    )


def dot(a, b):
    return jnp.dot(a, b, preferred_element_type=F32)


def dot_t(a, b):
    return lax.dot_general(a, b, (((1,), (1,)), ((), ())), preferred_element_type=F32)


def column_sums(a, b):
    return jnp.concatenate(
        [jnp.sum(a, axis=0, keepdims=True), jnp.sum(b, axis=0, keepdims=True)], axis=0
    )


class Plan:
    def __init__(self, n, m, samples, places, width, mid):
        self.n, self.m = n, m
        self.rows, self.width, self.mid = samples * places, width, mid
        self.counted = float(samples * places * n * m)
        steps = DILATION // places
        inner = 2
        while inner * inner < n:
            inner *= 2
        self.inner, self.nz, self.nx = inner, n // inner, inner // 2
        assert steps % inner == 0 and n % inner == 0
        self.hz = steps // inner
        assert 0 < self.hz < self.nz
        self.block = width // n
        self.padded = -(-self.block // 16) * 16
        if inner * m <= 8:
            self.phases = ("z", "plane")
        else:
            self.phases = ("z", "lo", "dp")
        size = {"plane": inner * m, "lo": inner, "dp": m, "z": self.nz}
        self.sizes = [size[p] for p in self.phases]
        self.slots = sum(s - 1 for s in self.sizes)
        q = self.nz * 2 - 1
        self.sems = 4 * self.slots + 4 * q + 2 * (self.nx * m - 1) + 2


def kernel(
    plan,
    x_hbm, cot_hbm, cw_hbm, pw_hbm, gi_hbm, bi_hbm, gm_hbm, bm_hbm,
    out_hbm, grad_hbm, convg_hbm, projg_hbm,
    x_ref, cot_ref, cw_ref, pw_ref, gi_ref, bi_ref, gm_ref, bm_ref,
    out_ref, grad_ref, convg_ref, projg_ref,
    src_w, src_m, got_w, got_m,
    act, h1, pre1, inner1, dact2, before, after, ysend, dact1,
    cot_t, act_t, cot_all, act_all, act2_all, dconv_all, part, parts, acc,
    send_sem, recv_sem, local_sem,
):
    n, m, nz, nx, inner = plan.n, plan.m, plan.nz, plan.nx, plan.inner
    rows, mid, width, block, padded = plan.rows, plan.mid, plan.width, plan.block, plan.padded
    me, dp = lax.axis_index("seq"), lax.axis_index("dp")
    z, lo = lax.div(me, inner), lax.rem(me, inner)
    xi, core = lax.div(lo, 2), lax.rem(lo, 2)
    loads = [
        pltpu.make_async_copy(a, b, local_sem.at[2 + i])
        for i, (a, b) in enumerate(
            (
                (x_hbm, x_ref), (cot_hbm, cot_ref), (pw_hbm, pw_ref), (gi_hbm, gi_ref),
                (bi_hbm, bi_ref), (cw_hbm, cw_ref), (gm_hbm, gm_ref), (bm_hbm, bm_ref),
            )
        )
    ]
    stores = [
        pltpu.make_async_copy(a, b, local_sem.at[10 + i])
        for i, (a, b) in enumerate(
            (
                (out_ref, out_hbm), (grad_ref, grad_hbm),
                (convg_ref, convg_hbm), (projg_ref, projg_hbm),
            )
        )
    ]
    for c in loads:
        c.start()
    counter = [0]
    pending = []

    def copy_to(src, dst, target):
        k = counter[0]
        counter[0] += 1
        return pltpu.make_async_remote_copy(
            src_ref=src, dst_ref=dst, send_sem=send_sem.at[k], recv_sem=recv_sem.at[k],
            device_id=target, device_id_type=MESH,
        )

    def push(src, dst, target):
        c = copy_to(src, dst, target)
        c.start()
        pending.append(c)
        return c

    def plane_peer(o):
        j = lax.rem(lo * m + dp + o, inner * m)
        return (z * inner + lax.div(j, m), lax.rem(j, m))

    def z_peer(o, c=None):
        c = core if c is None else c
        return (lax.rem(z + o, nz) * inner + xi * 2 + c, dp)

    peers = {
        "plane": plane_peer,
        "lo": lambda o: (z * inner + lax.rem(lo + o, inner), dp),
        "dp": lambda o: (me, lax.rem(dp + o, m)),
        "z": z_peer,
    }
    core_peer = (z * inner + xi * 2 + (1 - core), dp)

    def reduce_start(src, got, which):
        state = dict(src=src, got=got, which=which, phase=0, base=0)
        launch(state)
        return state

    def launch(st):
        ph = st["phase"]
        st["copies"] = [
            push(st["src"].at[st["which"], ph], st["got"].at[st["which"], st["base"] + o - 1],
                 peers[plan.phases[ph]](o))
            for o in range(1, plan.sizes[ph])
        ]

    def collect(st):
        ph = st["phase"]
        total = st["src"][st["which"], ph]
        for i, c in enumerate(st["copies"]):
            c.wait_recv()
            total = total + st["got"][st["which"], st["base"] + i]
        st["base"] += plan.sizes[ph] - 1
        st["phase"] += 1
        return total

    def reduce_step(st):
        total = collect(st)
        st["src"][st["which"], st["phase"]] = total
        launch(st)

    def reduce_mid(st):
        while st["phase"] < len(plan.phases) - 1:
            reduce_step(st)

    def reduce_end(st):
        reduce_mid(st)
        return collect(st) / plan.counted

    barrier = pltpu.get_barrier_semaphore()
    friends = [plane_peer(o) for o in range(1, inner * m)]
    friends += [z_peer(o, c) for o in range(1, nz) for c in (core, 1 - core)]
    for f in friends:
        pl.semaphore_signal(barrier, inc=1, device_id=f, device_id_type=MESH)

    loads[0].wait()
    x = x_ref[...].astype(F32)
    src_w[0, 0] = column_sums(x, x * x)
    pl.semaphore_wait(barrier, len(friends))
    red = reduce_start(src_w, got_w, 0)

    def stage_columns(value, staged):
        turned = value.T
        if padded != block:
            staged[...] = jnp.zeros_like(staged)
        for i in range(n):
            staged[i // inner, (i % inner) // 2, i % 2, :block, :] = turned[
                i * block : (i + 1) * block, :
            ].astype(BF16)

    def spread_columns(staged, gathered, sem):
        q = z * 2 + core
        lanes = pl.ds(pl.multiple_of(q * rows, rows), rows)
        own = pltpu.make_async_copy(staged.at[z, :, core], gathered.at[:, :, lanes], sem)
        own.start()
        copies = []
        for o in range(nz):
            for c in (core, 1 - core):
                if o == 0 and c is core:
                    continue
                copies.append(
                    push(staged.at[lax.rem(z + o, nz), :, c], gathered.at[:, :, lanes], z_peer(o, c))
                )
        return copies, own

    loads[1].wait()
    loads[2].wait()
    cot = cot_ref[...]
    stage_columns(cot.astype(F32), cot_t)
    reduce_step(red)
    cot_copies, own_cot = spread_columns(cot_t, cot_all, local_sem.at[0])
    dact2[...] = dot_t(cot_ref[...], pw_ref[...])
    for c in loads[3:]:
        c.wait()

    mean = reduce_end(red)
    center = mean[0:1]
    rs1 = 1.0 / jnp.sqrt(mean[1:2] - center * center + EPS)
    h = (x_ref[...].astype(F32) - center) * rs1
    h1[...] = h
    pre = gi_ref[...].reshape(1, -1) * h + bi_ref[...].reshape(1, -1)
    t = gelu_inner(pre)
    pre1[...] = pre
    inner1[...] = t
    act[...] = (0.5 * pre * (1.0 + t)).astype(BF16)

    steps = plan.hz * inner
    up = copy_to(ysend.at[0], before, (lax.rem(me + steps, n), dp))
    down = copy_to(ysend.at[1], after, (lax.rem(me + n - steps, n), dp))
    has_next, has_prev = me < n - steps, me >= steps

    @pl.when(has_next)
    def _():
        ysend[0] = dot(act[...], cw_ref[:, :mid]).astype(BF16)
        up.start()

    @pl.when(has_prev)
    def _():
        ysend[1] = dot(act[...], cw_ref[:, 2 * mid :]).astype(BF16)
        down.start()

    conv = dot(act[...], cw_ref[:, mid : 2 * mid])
    stage_columns(act[...].astype(F32), act_t)

    @pl.when(has_prev)
    def _():
        up.wait_recv()

    @pl.when(jnp.logical_not(has_prev))
    def _():
        before[...] = jnp.zeros_like(before)

    @pl.when(has_next)
    def _():
        down.wait_recv()

    @pl.when(jnp.logical_not(has_next))
    def _():
        after[...] = jnp.zeros_like(after)

    conv = conv + before[...].astype(F32) + after[...].astype(F32)
    src_m[0, 0] = column_sums(conv, conv * conv)
    red = reduce_start(src_m, got_m, 0)
    pre1[...] = gelu_slope(pre1[...], inner1[...])
    reduce_step(red)
    act_copies, own_act = spread_columns(act_t, act_all, local_sem.at[1])
    mean = reduce_end(red)
    center = mean[0:1]
    rs2 = 1.0 / jnp.sqrt(mean[1:2] - center * center + EPS)
    h2 = (conv - center) * rs2
    pre2 = gm_ref[...].reshape(1, -1) * h2 + bm_ref[...].reshape(1, -1)
    t2 = gelu_inner(pre2)
    act2 = (0.5 * pre2 * (1.0 + t2)).astype(BF16)
    dpre2 = dact2[...] * gelu_slope(pre2, t2)
    src_m[1, 0] = column_sums(dpre2, dpre2 * h2)
    red = reduce_start(src_m, got_m, 1)

    def place(zz, c):
        return pl.ds(pl.multiple_of((zz * 2 + c) * rows, rows), rows)

    own = place(z, core)

    def gather_start(full):
        order = sorted(range(1, nz), key=lambda o: o not in (plan.hz, nz - plan.hz))
        over_z = {o: push(full.at[own], full.at[own], z_peer(o)) for o in order}
        return over_z, [push(full.at[own], full.at[own], core_peer)]

    def pass_on(full, over_z, across, o):
        over_z[o].wait_recv()
        piece = full.at[place(lax.rem(z + nz - o, nz), core)]
        across.append(push(piece, piece, core_peer))

    act2_all[own, :] = act2
    reduce_step(red)
    act2_z, act2_c = gather_start(act2_all)
    out_ref[...] = (x_ref[...].astype(F32) + dot(act2, pw_ref[...])).astype(BF16)
    stores[0].start()
    mean = reduce_end(red)
    dconv = (gm_ref[...].reshape(1, -1) * (dpre2 - mean[0:1] - h2 * mean[1:2]) * rs2).astype(BF16)
    dconv_all[own, :] = dconv
    dconv_z, dconv_c = gather_start(dconv_all)
    dact1[...] = dot_t(dconv, cw_ref[:, mid : 2 * mid])
    for o in range(1, nz):
        pass_on(act2_all, act2_z, act2_c, o)
    halo = sorted({plan.hz, nz - plan.hz})
    for o in halo:
        pass_on(dconv_all, dconv_z, dconv_c, o)

    @pl.when(z + plan.hz < nz)
    def _():
        dact1[...] += dot_t(
            dconv_all[place(lax.rem(z + plan.hz, nz), core), :], cw_ref[:, :mid]
        )

    @pl.when(z >= plan.hz)
    def _():
        dact1[...] += dot_t(
            dconv_all[place(lax.rem(z + nz - plan.hz, nz), core), :], cw_ref[:, 2 * mid :]
        )

    dpre1 = dact1[...] * pre1[...]
    dact1[...] = dpre1
    src_w[1, 0] = column_sums(dpre1, dpre1 * h1[...])
    red = reduce_start(src_w, got_w, 1)

    group = nx * m
    mine = xi * m + dp

    def send_parts(columns):
        copies = []
        for o in range(1, group):
            to = lax.rem(mine + o, group)
            tx, ty = lax.div(to, m), lax.rem(to, m)
            copies.append(
                push(
                    part.at[tx, :, columns],
                    parts.at[mine, :, columns],
                    (z * inner + tx * 2 + core, ty),
                )
            )
        parts[pl.ds(mine, 1), :, columns] = part[pl.ds(xi, 1), :, columns]
        return copies

    own_cot.wait()
    for c in cot_copies + act2_c:
        c.wait_recv()
    for k in range(nx):
        part[k, :, 3 * mid :] = dot(cot_all[k], act2_all[...]).astype(BF16)
    acc[...] = jnp.zeros_like(acc)
    own_act.wait()
    for c in act_copies:
        c.wait_recv()

    def add_plane(o, passed):
        dconv_c[passed].wait_recv()
        p = lax.rem(z + nz - o, nz)
        span = 2 * rows
        g = dconv_all[pl.ds(pl.multiple_of(p * span, span), span), :]

        def add(tap, q):
            a = act_all[:, :, pl.ds(pl.multiple_of(q * span, span), span)]
            acc[:, tap * mid : (tap + 1) * mid] += dot(a.reshape(nx * padded, span), g)

        add(1, p)

        @pl.when(p >= plan.hz)
        def _():
            add(0, p - plan.hz)

        @pl.when(p + plan.hz < nz)
        def _():
            add(2, p + plan.hz)

    add_plane(0, 0)
    for i, o in enumerate(halo):
        add_plane(o, 1 + i)
    reduce_mid(red)
    part_copies = send_parts(pl.ds(3 * mid, mid))
    rest = [o for o in range(1, nz) if o not in halo]
    for o in rest:
        pass_on(dconv_all, dconv_z, dconv_c, o)
    for i, o in enumerate(rest):
        add_plane(o, 1 + len(halo) + i)
    part[:, :, : 3 * mid] = acc[...].reshape(nx, padded, 3 * mid).astype(BF16)
    part_copies += send_parts(pl.ds(0, 3 * mid))

    mean = reduce_end(red)
    grad_ref[...] = (
        cot_ref[...].astype(F32)
        + gi_ref[...].reshape(1, -1) * (dact1[...] - mean[0:1] - h1[...] * mean[1:2]) * rs1
    ).astype(BF16)
    stores[1].start()

    for c in part_copies:
        c.wait_recv()
    total = parts[0].astype(F32)
    for k in range(1, group):
        total = total + parts[k].astype(F32)
    convg_ref[...] = total[:block, : 3 * mid]
    projg_ref[...] = total[:block, 3 * mid :]
    stores[2].start()
    stores[3].start()
    for c in stores:
        c.wait()

    for c in pending:
        c.wait_send()

    @pl.when(has_next)
    def _():
        up.wait_send()

    @pl.when(has_prev)
    def _():
        down.wait_send()


def copy_kernel(count, *refs):
    for i in range(count):
        refs[count + i][...] = refs[i][...]


def per_device(inputs, cotangent, conv_weight, proj_weight, gain_in, bias_in, gain_mid, bias_mid):
    samples, places, width = inputs.shape
    mid = proj_weight.shape[0]
    plan = Plan(
        lax.axis_size("seq"), lax.axis_size("dp"), samples, places, width, mid
    )
    rows, nz, nx, padded = plan.rows, plan.nz, plan.nx, plan.padded
    depth = nz * 2 * rows
    hbm = pl.BlockSpec(memory_space=pl.ANY)
    vmem = pl.BlockSpec(memory_space=pltpu.VMEM)
    outs = (
        jax.ShapeDtypeStruct((rows, width), BF16),
        jax.ShapeDtypeStruct((rows, width), BF16),
        jax.ShapeDtypeStruct((plan.block, 3 * mid), F32),
        jax.ShapeDtypeStruct((plan.block, mid), F32),
    )
    phases = len(plan.phases)
    results = pl.pallas_call(
        functools.partial(kernel, plan),
        out_shape=outs,
        in_specs=[hbm] * 8,
        out_specs=(hbm,) * 4,
        scratch_shapes=[
            pltpu.VMEM((rows, width), BF16),
            pltpu.VMEM((rows, width), BF16),
            pltpu.VMEM((width, 3 * mid), BF16),
            pltpu.VMEM((mid, width), BF16),
            pltpu.VMEM((width,), F32),
            pltpu.VMEM((width,), F32),
            pltpu.VMEM((mid,), F32),
            pltpu.VMEM((mid,), F32),
            *[pltpu.VMEM(o.shape, o.dtype) for o in outs],
            pltpu.VMEM((2, phases, 2, width), F32),
            pltpu.VMEM((2, phases, 2, mid), F32),
            pltpu.VMEM((2, plan.slots, 2, width), F32),
            pltpu.VMEM((2, plan.slots, 2, mid), F32),
            pltpu.VMEM((rows, width), BF16),
            pltpu.VMEM((rows, width), F32),
            pltpu.VMEM((rows, width), F32),
            pltpu.VMEM((rows, width), F32),
            pltpu.VMEM((rows, mid), F32),
            pltpu.VMEM((rows, mid), BF16),
            pltpu.VMEM((rows, mid), BF16),
            pltpu.VMEM((2, rows, mid), BF16),
            pltpu.VMEM((rows, width), F32),
            pltpu.VMEM((nz, nx, 2, padded, rows), BF16),
            pltpu.VMEM((nz, nx, 2, padded, rows), BF16),
            pltpu.VMEM((nx, padded, depth), BF16),
            pltpu.VMEM((nx, padded, depth), BF16),
            pltpu.VMEM((depth, mid), BF16),
            pltpu.VMEM((depth, mid), BF16),
            pltpu.VMEM((nx, padded, 4 * mid), BF16),
            pltpu.VMEM((nx * plan.m, padded, 4 * mid), BF16),
            pltpu.VMEM((nx * padded, 3 * mid), F32),
            pltpu.SemaphoreType.DMA((plan.sems,)),
            pltpu.SemaphoreType.DMA((plan.sems,)),
            pltpu.SemaphoreType.DMA((14,)),
        ],
        compiler_params=pltpu.CompilerParams(
            collective_id=0, has_side_effects=True, vmem_limit_bytes=56 * 1024 * 1024
        ),
    )(
        inputs.reshape(rows, width),
        cotangent.reshape(rows, width),
        conv_weight,
        proj_weight,
        gain_in,
        bias_in,
        gain_mid,
        bias_mid,
    )
    block_out, input_grad, conv_grad, proj_grad = pl.pallas_call(
        functools.partial(copy_kernel, len(outs)),
        out_shape=outs,
        in_specs=[vmem] * len(outs),
        out_specs=(vmem,) * len(outs),
        compiler_params=pltpu.CompilerParams(vmem_limit_bytes=56 * 1024 * 1024),
    )(*results)
    shape = (samples, places, width)
    return (block_out.reshape(shape), input_grad.reshape(shape), conv_grad, proj_grad)


def solution(mesh):
    in_specs = (P("dp", "seq", None), P("dp", "seq", None), P(), P(), P(), P(), P(), P())
    out_specs = (P("dp", "seq", None), P("dp", "seq", None), P("seq", None), P("seq", None))
    return jax.shard_map(
        per_device, mesh=mesh, in_specs=in_specs, out_specs=out_specs, check_vma=False
    )
```

```python
import functools
import math

import jax
import jax.numpy as jnp
from jax import lax
from jax.experimental import pallas as pl
from jax.experimental.pallas import tpu as pltpu
from jax.sharding import PartitionSpec as P

DILATION = 1024
EPS = 1e-05
EXTRA = 16
COEFF = math.sqrt(2.0 / math.pi)
MESH = pl.DeviceIdType.MESH
F32, BF16 = jnp.float32, jnp.bfloat16


def gelu_inner(v):
    return jnp.tanh(COEFF * (v + 0.044715 * v * v * v))


def gelu_slope(v, inner):
    return 0.5 * (1.0 + inner) + 0.5 * v * (1.0 - inner * inner) * COEFF * (
        1.0 + 3.0 * 0.044715 * v * v
    )


def dot(a, b):
    return jnp.dot(a, b, preferred_element_type=F32)


def dot_t(a, b):
    return lax.dot_general(a, b, (((1,), (1,)), ((), ())), preferred_element_type=F32)


def column_sums(a, b):
    return jnp.concatenate(
        [jnp.sum(a, axis=0, keepdims=True), jnp.sum(b, axis=0, keepdims=True)], axis=0
    )


def packed(v):
    m = jnp.mean(v, axis=0, keepdims=True)
    high = m.astype(BF16).astype(F32)
    mid = (m - high).astype(BF16).astype(F32)
    low = m - high - mid
    pad = jnp.zeros((EXTRA - 3, v.shape[1]), F32)
    return jnp.concatenate([v - m, high, mid, low, pad], axis=0).astype(BF16)


def unpacked(v):
    f = v.astype(F32)
    r = v.shape[0] - EXTRA
    return f[:r] + (f[r : r + 1] + f[r + 1 : r + 2] + f[r + 2 : r + 3])


class Plan:
    def __init__(self, n, m, samples, places, width, mid):
        self.n, self.m = n, m
        self.rows, self.width, self.mid = samples * places, width, mid
        self.counted = float(samples * places * n * m)
        steps = DILATION // places
        inner = 2
        while inner * inner < n:
            inner *= 2
        self.inner, self.nz, self.nx = inner, n // inner, inner // 2
        assert steps % inner == 0 and n % inner == 0
        self.hz = steps // inner
        assert 0 < self.hz < self.nz
        self.block = width // n
        self.padded = -(-self.block // 16) * 16
        if inner * m <= 8:
            self.phases = ("z", "plane")
        else:
            self.phases = ("z", "lo", "dp")
        size = {"plane": inner * m, "lo": inner, "dp": m, "z": self.nz}
        self.sizes = [size[p] for p in self.phases]
        self.slots = sum(s - 1 for s in self.sizes)
        q = self.nz * 2 - 1
        self.sems = 4 * self.slots + 4 * q + 2 * (self.nx * m - 1) + 2


def kernel(
    plan,
    x_hbm, cot_hbm, cw_hbm, pw_hbm, gi_hbm, bi_hbm, gm_hbm, bm_hbm,
    out_hbm, grad_hbm, convg_hbm, projg_hbm,
    x_ref, cot_ref, cw_ref, pw_ref, gi_ref, bi_ref, gm_ref, bm_ref,
    out_ref, grad_ref, convg_ref, projg_ref,
    src_w, src_m, got_w, got_m,
    act, h1, pre1, inner1, dact2, before, after, ysend, dact1,
    cot_t, act_t, cot_all, act_all, act2_all, dconv_all, dact_all, conv_all, part, parts, acc,
    send_sem, recv_sem, local_sem,
):
    n, m, nz, nx, inner = plan.n, plan.m, plan.nz, plan.nx, plan.inner
    rows, mid, width, block, padded = plan.rows, plan.mid, plan.width, plan.block, plan.padded
    me, dp = lax.axis_index("seq"), lax.axis_index("dp")
    z, lo = lax.div(me, inner), lax.rem(me, inner)
    xi, core = lax.div(lo, 2), lax.rem(lo, 2)
    loads = [
        pltpu.make_async_copy(a, b, local_sem.at[2 + i])
        for i, (a, b) in enumerate(
            (
                (x_hbm, x_ref), (cot_hbm, cot_ref), (pw_hbm, pw_ref), (gi_hbm, gi_ref),
                (bi_hbm, bi_ref), (cw_hbm, cw_ref), (gm_hbm, gm_ref), (bm_hbm, bm_ref),
            )
        )
    ]
    stores = [
        pltpu.make_async_copy(a, b, local_sem.at[10 + i])
        for i, (a, b) in enumerate(
            (
                (out_ref, out_hbm), (grad_ref, grad_hbm),
                (convg_ref, convg_hbm), (projg_ref, projg_hbm),
            )
        )
    ]
    for c in loads:
        c.start()
    counter = [0]
    pending = []

    def copy_to(src, dst, target):
        k = counter[0]
        counter[0] += 1
        return pltpu.make_async_remote_copy(
            src_ref=src, dst_ref=dst, send_sem=send_sem.at[k], recv_sem=recv_sem.at[k],
            device_id=target, device_id_type=MESH,
        )

    def push(src, dst, target):
        c = copy_to(src, dst, target)
        c.start()
        pending.append(c)
        return c

    def plane_peer(o):
        j = lax.rem(lo * m + dp + o, inner * m)
        return (z * inner + lax.div(j, m), lax.rem(j, m))

    def z_peer(o, c=None):
        c = core if c is None else c
        return (lax.rem(z + o, nz) * inner + xi * 2 + c, dp)

    peers = {
        "plane": plane_peer,
        "lo": lambda o: (z * inner + lax.rem(lo + o, inner), dp),
        "dp": lambda o: (me, lax.rem(dp + o, m)),
        "z": z_peer,
    }
    core_peer = (z * inner + xi * 2 + (1 - core), dp)

    def reduce_start(src, got, which):
        state = dict(src=src, got=got, which=which, phase=0, base=0)
        launch(state)
        return state

    def launch(st):
        ph = st["phase"]
        st["copies"] = [
            push(st["src"].at[st["which"], ph], st["got"].at[st["which"], st["base"] + o - 1],
                 peers[plan.phases[ph]](o))
            for o in range(1, plan.sizes[ph])
        ]

    def collect(st):
        ph = st["phase"]
        total = st["src"][st["which"], ph]
        for i, c in enumerate(st["copies"]):
            c.wait_recv()
            total = total + st["got"][st["which"], st["base"] + i]
        st["base"] += plan.sizes[ph] - 1
        st["phase"] += 1
        return total

    def reduce_step(st):
        total = collect(st)
        st["src"][st["which"], st["phase"]] = total
        launch(st)

    def reduce_mid(st):
        while st["phase"] < len(plan.phases) - 1:
            reduce_step(st)

    def reduce_end(st):
        reduce_mid(st)
        return collect(st) / plan.counted

    barrier = pltpu.get_barrier_semaphore()
    friends = [plane_peer(o) for o in range(1, inner * m)]
    friends += [z_peer(o, c) for o in range(1, nz) for c in (core, 1 - core)]
    for f in friends:
        pl.semaphore_signal(barrier, inc=1, device_id=f, device_id_type=MESH)

    loads[0].wait()
    x = x_ref[...].astype(F32)
    src_w[0, 0] = column_sums(x, x * x)
    pl.semaphore_wait(barrier, len(friends))
    red = reduce_start(src_w, got_w, 0)

    def stage_columns(value, staged):
        turned = value.T
        if padded != block:
            staged[...] = jnp.zeros_like(staged)
        for i in range(n):
            staged[i // inner, (i % inner) // 2, i % 2, :block, :] = turned[
                i * block : (i + 1) * block, :
            ].astype(BF16)

    def spread_columns(staged, gathered, sem):
        q = z * 2 + core
        lanes = pl.ds(pl.multiple_of(q * rows, rows), rows)
        own = pltpu.make_async_copy(staged.at[z, :, core], gathered.at[:, :, lanes], sem)
        own.start()
        copies = []
        for o in range(nz):
            for c in (core, 1 - core):
                if o == 0 and c is core:
                    continue
                copies.append(
                    push(staged.at[lax.rem(z + o, nz), :, c], gathered.at[:, :, lanes], z_peer(o, c))
                )
        return copies, own

    def place(zz, c, size=rows):
        return pl.ds(pl.multiple_of((zz * 2 + c) * size, size), size)

    long = rows + EXTRA
    own = place(z, core)
    halo = sorted({plan.hz, nz - plan.hz})
    rest = [o for o in range(1, nz) if o not in halo]

    def gather_start(full, size):
        at = full.at[place(z, core, size)]
        over_z = {o: push(at, at, z_peer(o)) for o in halo + rest}
        return over_z, {0: push(at, at, core_peer)}

    def pass_on(full, size, over_z, across, o):
        over_z[o].wait_recv()
        piece = full.at[place(lax.rem(z + nz - o, nz), core, size)]
        across[o] = push(piece, piece, core_peer)

    loads[1].wait()
    loads[2].wait()
    dact = dot_t(cot_ref[...], pw_ref[...])
    dact2[...] = dact
    dact_all[own, :] = dact.astype(BF16)
    reduce_step(red)
    dact_z, dact_c = gather_start(dact_all, rows)
    stage_columns(cot_ref[...].astype(F32), cot_t)
    for c in loads[3:]:
        c.wait()

    mean = reduce_end(red)
    center = mean[0:1]
    rs1 = 1.0 / jnp.sqrt(mean[1:2] - center * center + EPS)
    h = (x_ref[...].astype(F32) - center) * rs1
    h1[...] = h
    pre = gi_ref[...].reshape(1, -1) * h + bi_ref[...].reshape(1, -1)
    t = gelu_inner(pre)
    pre1[...] = pre
    inner1[...] = t
    act[...] = (0.5 * pre * (1.0 + t)).astype(BF16)

    steps = plan.hz * inner
    up = copy_to(ysend.at[0], before, (lax.rem(me + steps, n), dp))
    down = copy_to(ysend.at[1], after, (lax.rem(me + n - steps, n), dp))
    has_next, has_prev = me < n - steps, me >= steps

    @pl.when(has_next)
    def _():
        ysend[0] = packed(dot(act[...], cw_ref[:, :mid]))
        up.start()

    @pl.when(has_prev)
    def _():
        ysend[1] = packed(dot(act[...], cw_ref[:, 2 * mid :]))
        down.start()

    conv = dot(act[...], cw_ref[:, mid : 2 * mid])
    stage_columns(act[...].astype(F32), act_t)

    @pl.when(has_prev)
    def _():
        up.wait_recv()

    @pl.when(jnp.logical_not(has_prev))
    def _():
        before[...] = jnp.zeros_like(before)

    @pl.when(has_next)
    def _():
        down.wait_recv()

    @pl.when(jnp.logical_not(has_next))
    def _():
        after[...] = jnp.zeros_like(after)

    conv = conv + unpacked(before[...]) + unpacked(after[...])
    src_m[0, 0] = column_sums(conv, conv * conv)
    red = reduce_start(src_m, got_m, 0)
    conv_all[place(z, core, long), :] = packed(conv)
    for o in halo + rest:
        pass_on(dact_all, rows, dact_z, dact_c, o)
    reduce_step(red)
    conv_z, conv_c = gather_start(conv_all, long)
    pre1[...] = gelu_slope(pre1[...], inner1[...])
    act_copies, own_act = spread_columns(act_t, act_all, local_sem.at[1])
    mean = reduce_end(red)
    center = mean[0:1]
    rs2 = 1.0 / jnp.sqrt(mean[1:2] - center * center + EPS)
    h2 = (conv - center) * rs2
    pre2 = gm_ref[...].reshape(1, -1) * h2 + bm_ref[...].reshape(1, -1)
    t2 = gelu_inner(pre2)
    act2 = (0.5 * pre2 * (1.0 + t2)).astype(BF16)
    dpre2 = dact2[...] * gelu_slope(pre2, t2)
    src_m[1, 0] = column_sums(dpre2, dpre2 * h2)
    red = reduce_start(src_m, got_m, 1)

    act2_all[own, :] = act2
    out_ref[...] = (x_ref[...].astype(F32) + dot(act2, pw_ref[...])).astype(BF16)
    stores[0].start()
    reduce_step(red)
    cot_copies, own_cot = spread_columns(cot_t, cot_all, local_sem.at[0])
    for o in halo + rest:
        pass_on(conv_all, long, conv_z, conv_c, o)

    def remake(o, c):
        zz = lax.rem(z + nz - o, nz)
        h = (unpacked(conv_all[place(zz, c, long), :]) - center) * rs2
        pre = gm_ref[...].reshape(1, -1) * h + bm_ref[...].reshape(1, -1)
        t = gelu_inner(pre)
        act2_all[place(zz, c), :] = (0.5 * pre * (1.0 + t)).astype(BF16)
        return h, dact_all[place(zz, c), :].astype(F32) * gelu_slope(pre, t)

    def remake_dconv(o, c, h, d):
        zz = lax.rem(z + nz - o, nz)
        dconv_all[place(zz, c), :] = (scale2 * (d - mean2[0:1] - h * mean2[1:2])).astype(BF16)

    remade = {o: remake(o, core) for o in halo}
    mean2 = reduce_end(red)
    scale2 = gm_ref[...].reshape(1, -1) * rs2
    remake_dconv(0, core, h2, dpre2)
    for o in halo:
        remake_dconv(o, core, *remade[o])
    dact1[...] = dot_t(dconv_all[own, :], cw_ref[:, mid : 2 * mid])

    @pl.when(z + plan.hz < nz)
    def _():
        dact1[...] += dot_t(
            dconv_all[place(lax.rem(z + plan.hz, nz), core), :], cw_ref[:, :mid]
        )

    @pl.when(z >= plan.hz)
    def _():
        dact1[...] += dot_t(
            dconv_all[place(lax.rem(z + nz - plan.hz, nz), core), :], cw_ref[:, 2 * mid :]
        )

    dpre1 = dact1[...] * pre1[...]
    dact1[...] = dpre1
    src_w[1, 0] = column_sums(dpre1, dpre1 * h1[...])
    red = reduce_start(src_w, got_w, 1)

    group = nx * m
    mine = xi * m + dp

    def send_parts(columns):
        copies = []
        for o in range(1, group):
            to = lax.rem(mine + o, group)
            tx, ty = lax.div(to, m), lax.rem(to, m)
            copies.append(
                push(
                    part.at[tx, :, columns],
                    parts.at[mine, :, columns],
                    (z * inner + tx * 2 + core, ty),
                )
            )
        parts[pl.ds(mine, 1), :, columns] = part[pl.ds(xi, 1), :, columns]
        return copies

    acc[...] = jnp.zeros_like(acc)
    own_act.wait()
    for c in act_copies:
        c.wait_recv()

    def add_plane(o):
        p = lax.rem(z + nz - o, nz)
        span = 2 * rows
        g = dconv_all[pl.ds(pl.multiple_of(p * span, span), span), :]

        def add(tap, q):
            a = act_all[:, :, pl.ds(pl.multiple_of(q * span, span), span)]
            acc[:, tap * mid : (tap + 1) * mid] += dot(a.reshape(nx * padded, span), g)

        add(1, p)

        @pl.when(p >= plan.hz)
        def _():
            add(0, p - plan.hz)

        @pl.when(p + plan.hz < nz)
        def _():
            add(2, p + plan.hz)

    for o in rest:
        remake_dconv(o, core, *remake(o, core))
    for o in [0] + halo + rest:
        dact_c[o].wait_recv()
        conv_c[o].wait_recv()
        remake_dconv(o, 1 - core, *remake(o, 1 - core))
        add_plane(o)
    part[:, :, : 3 * mid] = acc[...].reshape(nx, padded, 3 * mid).astype(BF16)
    reduce_mid(red)
    part_copies = send_parts(pl.ds(0, 3 * mid))
    own_cot.wait()
    for c in cot_copies:
        c.wait_recv()
    for k in range(nx):
        part[k, :, 3 * mid :] = dot(cot_all[k], act2_all[...]).astype(BF16)
    part_copies += send_parts(pl.ds(3 * mid, mid))

    mean = reduce_end(red)
    grad_ref[...] = (
        cot_ref[...].astype(F32)
        + gi_ref[...].reshape(1, -1) * (dact1[...] - mean[0:1] - h1[...] * mean[1:2]) * rs1
    ).astype(BF16)
    stores[1].start()

    for c in part_copies:
        c.wait_recv()
    total = parts[0].astype(F32)
    for k in range(1, group):
        total = total + parts[k].astype(F32)
    convg_ref[...] = total[:block, : 3 * mid]
    projg_ref[...] = total[:block, 3 * mid :]
    stores[2].start()
    stores[3].start()
    for c in stores:
        c.wait()

    for c in pending:
        c.wait_send()

    @pl.when(has_next)
    def _():
        up.wait_send()

    @pl.when(has_prev)
    def _():
        down.wait_send()


def copy_kernel(count, *refs):
    for i in range(count):
        refs[count + i][...] = refs[i][...]


def per_device(inputs, cotangent, conv_weight, proj_weight, gain_in, bias_in, gain_mid, bias_mid):
    samples, places, width = inputs.shape
    mid = proj_weight.shape[0]
    plan = Plan(
        lax.axis_size("seq"), lax.axis_size("dp"), samples, places, width, mid
    )
    rows, nz, nx, padded = plan.rows, plan.nz, plan.nx, plan.padded
    depth = nz * 2 * rows
    hbm = pl.BlockSpec(memory_space=pl.ANY)
    vmem = pl.BlockSpec(memory_space=pltpu.VMEM)
    outs = (
        jax.ShapeDtypeStruct((rows, width), BF16),
        jax.ShapeDtypeStruct((rows, width), BF16),
        jax.ShapeDtypeStruct((plan.block, 3 * mid), F32),
        jax.ShapeDtypeStruct((plan.block, mid), F32),
    )
    phases = len(plan.phases)
    results = pl.pallas_call(
        functools.partial(kernel, plan),
        out_shape=outs,
        in_specs=[hbm] * 8,
        out_specs=(hbm,) * 4,
        scratch_shapes=[
            pltpu.VMEM((rows, width), BF16),
            pltpu.VMEM((rows, width), BF16),
            pltpu.VMEM((width, 3 * mid), BF16),
            pltpu.VMEM((mid, width), BF16),
            pltpu.VMEM((width,), F32),
            pltpu.VMEM((width,), F32),
            pltpu.VMEM((mid,), F32),
            pltpu.VMEM((mid,), F32),
            *[pltpu.VMEM(o.shape, o.dtype) for o in outs],
            pltpu.VMEM((2, phases, 2, width), F32),
            pltpu.VMEM((2, phases, 2, mid), F32),
            pltpu.VMEM((2, plan.slots, 2, width), F32),
            pltpu.VMEM((2, plan.slots, 2, mid), F32),
            pltpu.VMEM((rows, width), BF16),
            pltpu.VMEM((rows, width), F32),
            pltpu.VMEM((rows, width), F32),
            pltpu.VMEM((rows, width), F32),
            pltpu.VMEM((rows, mid), F32),
            pltpu.VMEM((rows + EXTRA, mid), BF16),
            pltpu.VMEM((rows + EXTRA, mid), BF16),
            pltpu.VMEM((2, rows + EXTRA, mid), BF16),
            pltpu.VMEM((rows, width), F32),
            pltpu.VMEM((nz, nx, 2, padded, rows), BF16),
            pltpu.VMEM((nz, nx, 2, padded, rows), BF16),
            pltpu.VMEM((nx, padded, depth), BF16),
            pltpu.VMEM((nx, padded, depth), BF16),
            pltpu.VMEM((depth, mid), BF16),
            pltpu.VMEM((depth, mid), BF16),
            pltpu.VMEM((depth, mid), BF16),
            pltpu.VMEM((nz * 2 * (rows + EXTRA), mid), BF16),
            pltpu.VMEM((nx, padded, 4 * mid), BF16),
            pltpu.VMEM((nx * plan.m, padded, 4 * mid), BF16),
            pltpu.VMEM((nx * padded, 3 * mid), F32),
            pltpu.SemaphoreType.DMA((plan.sems,)),
            pltpu.SemaphoreType.DMA((plan.sems,)),
            pltpu.SemaphoreType.DMA((14,)),
        ],
        compiler_params=pltpu.CompilerParams(
            collective_id=0, has_side_effects=True, vmem_limit_bytes=56 * 1024 * 1024
        ),
    )(
        inputs.reshape(rows, width),
        cotangent.reshape(rows, width),
        conv_weight,
        proj_weight,
        gain_in,
        bias_in,
        gain_mid,
        bias_mid,
    )
    block_out, input_grad, conv_grad, proj_grad = pl.pallas_call(
        functools.partial(copy_kernel, len(outs)),
        out_shape=outs,
        in_specs=[vmem] * len(outs),
        out_specs=(vmem,) * len(outs),
        compiler_params=pltpu.CompilerParams(vmem_limit_bytes=56 * 1024 * 1024),
    )(*results)
    shape = (samples, places, width)
    return (block_out.reshape(shape), input_grad.reshape(shape), conv_grad, proj_grad)


def solution(mesh):
    in_specs = (P("dp", "seq", None), P("dp", "seq", None), P(), P(), P(), P(), P(), P())
    out_specs = (P("dp", "seq", None), P("dp", "seq", None), P("seq", None), P("seq", None))
    return jax.shard_map(
        per_device, mesh=mesh, in_specs=in_specs, out_specs=out_specs, check_vma=False
    )
```

```python
import functools
import math

import jax
import jax.numpy as jnp
from jax import lax
from jax.experimental import pallas as pl
from jax.experimental.pallas import tpu as pltpu
from jax.sharding import PartitionSpec as P

DILATION = 1024
EPS = 1e-05
EXTRA = 16
COEFF = math.sqrt(2.0 / math.pi)
MESH = pl.DeviceIdType.MESH
F32, BF16 = jnp.float32, jnp.bfloat16


def gelu_inner(v):
    return jnp.tanh(COEFF * (v + 0.044715 * v * v * v))


def gelu_slope(v, inner):
    return 0.5 * (1.0 + inner) + 0.5 * v * (1.0 - inner * inner) * COEFF * (
        1.0 + 3.0 * 0.044715 * v * v
    )


def dot(a, b):
    return jnp.dot(a, b, preferred_element_type=F32)


def dot_t(a, b):
    return lax.dot_general(a, b, (((1,), (1,)), ((), ())), preferred_element_type=F32)


def column_sums(a, b):
    return jnp.concatenate(
        [jnp.sum(a, axis=0, keepdims=True), jnp.sum(b, axis=0, keepdims=True)], axis=0
    )


def packed(v):
    m = jnp.mean(v, axis=0, keepdims=True)
    high = m.astype(BF16).astype(F32)
    mid = (m - high).astype(BF16).astype(F32)
    low = m - high - mid
    pad = jnp.zeros((EXTRA - 3, v.shape[1]), F32)
    return jnp.concatenate([v - m, high, mid, low, pad], axis=0).astype(BF16)


def unpacked(v):
    f = v.astype(F32)
    r = v.shape[0] - EXTRA
    return f[:r] + (f[r : r + 1] + f[r + 1 : r + 2] + f[r + 2 : r + 3])


def fold(v):
    return jnp.sum(v.reshape(v.shape[0] // 8, 8, v.shape[1]), axis=0)


def each(count, size, body):
    def step(i, carry):
        new = body(pl.ds(pl.multiple_of(i * size, size), size), i * size)
        return tuple(a + fold(b) for a, b in zip(carry, new or ()))

    def run(width=None):
        init = () if width is None else (jnp.zeros((8, width), F32),) * 2
        return lax.fori_loop(0, count // size, step, init)

    return run


class Plan:
    def __init__(self, n, m, samples, places, width, mid):
        self.n, self.m = n, m
        self.rows, self.width, self.mid = samples * places, width, mid
        self.counted = float(samples * places * n * m)
        steps = DILATION // places
        inner = 2
        while inner * inner < n:
            inner *= 2
        self.inner, self.nz, self.nx = inner, n // inner, inner // 2
        assert steps % inner == 0 and n % inner == 0
        self.hz = steps // inner
        assert 0 < self.hz < self.nz
        self.block = width // n
        self.padded = -(-self.block // 16) * 16
        if n * m <= 32:
            self.phases = ("core", "chips")
        else:
            self.phases = ("z", "lo", "dp")
        size = {"core": 2, "chips": n * m // 2, "lo": inner, "dp": m, "z": self.nz}
        self.sizes = [size[p] for p in self.phases]
        self.slots = sum(s - 1 for s in self.sizes)
        q = self.nz * 2 - 1
        self.sems = 4 * self.slots + 4 * q + 2 * (self.nx * m - 1) + 2


def kernel(
    plan,
    x_hbm, cot_hbm, cw_hbm, pw_hbm, gi_hbm, bi_hbm, gm_hbm, bm_hbm,
    out_hbm, grad_hbm, convg_hbm, projg_hbm,
    x_ref, cot_ref, cw_ref, pw_ref, gi_ref, bi_ref, gm_ref, bm_ref,
    out_ref, grad_ref, convg_ref, projg_ref,
    src_w, src_m, got_w, got_m,
    act, h1, slope1, mids, dact2, before, after, ysend, dact1,
    cot_t, act_t, cot_all, act_all, act2_all, dconv_all, dact_all, conv_all, part, parts, acc, stacked, kept,
    send_sem, recv_sem, local_sem,
):
    n, m, nz, nx, inner = plan.n, plan.m, plan.nz, plan.nx, plan.inner
    rows, mid, width, block, padded = plan.rows, plan.mid, plan.width, plan.block, plan.padded
    me, dp = lax.axis_index("seq"), lax.axis_index("dp")
    z, lo = lax.div(me, inner), lax.rem(me, inner)
    xi, core = lax.div(lo, 2), lax.rem(lo, 2)
    loads = [
        pltpu.make_async_copy(a, b, local_sem.at[2 + i])
        for i, (a, b) in enumerate(
            (
                (x_hbm, x_ref), (cot_hbm, cot_ref), (pw_hbm, pw_ref), (gi_hbm, gi_ref),
                (bi_hbm, bi_ref), (cw_hbm, cw_ref), (gm_hbm, gm_ref), (bm_hbm, bm_ref),
            )
        )
    ]
    stores = [
        pltpu.make_async_copy(a, b, local_sem.at[10 + i])
        for i, (a, b) in enumerate(
            (
                (out_ref, out_hbm), (grad_ref, grad_hbm),
                (convg_ref, convg_hbm), (projg_ref, projg_hbm),
            )
        )
    ]
    for c in loads:
        c.start()
    counter = [0]
    pending = []

    def copy_to(src, dst, target):
        k = counter[0]
        counter[0] += 1
        return pltpu.make_async_remote_copy(
            src_ref=src, dst_ref=dst, send_sem=send_sem.at[k], recv_sem=recv_sem.at[k],
            device_id=target, device_id_type=MESH,
        )

    def push(src, dst, target):
        c = copy_to(src, dst, target)
        c.start()
        pending.append(c)
        return c

    def plane_peer(o):
        j = lax.rem(lo * m + dp + o, inner * m)
        return (z * inner + lax.div(j, m), lax.rem(j, m))

    def z_peer(o, c=None):
        c = core if c is None else c
        return (lax.rem(z + o, nz) * inner + xi * 2 + c, dp)

    def chip_peer(o):
        j = lax.rem((z * nx + xi) * m + dp + o, n * m // 2)
        return (lax.div(j, m) * 2 + core, lax.rem(j, m))

    peers = {
        "core": lambda o: core_peer,
        "chips": chip_peer,
        "lo": lambda o: (z * inner + lax.rem(lo + o, inner), dp),
        "dp": lambda o: (me, lax.rem(dp + o, m)),
        "z": z_peer,
    }
    core_peer = (z * inner + xi * 2 + (1 - core), dp)

    def reduce_start(src, got, which):
        state = dict(src=src, got=got, which=which, phase=0, base=0)
        launch(state)
        return state

    def launch(st):
        ph = st["phase"]
        st["copies"] = [
            push(st["src"].at[st["which"], ph], st["got"].at[st["which"], st["base"] + o - 1],
                 peers[plan.phases[ph]](o))
            for o in range(1, plan.sizes[ph])
        ]

    def collect(st):
        ph = st["phase"]
        total = st["src"][st["which"], ph]
        for i, c in enumerate(st["copies"]):
            c.wait_recv()
            total = total + st["got"][st["which"], st["base"] + i]
        st["base"] += plan.sizes[ph] - 1
        st["phase"] += 1
        return total

    def reduce_step(st):
        total = collect(st)
        st["src"][st["which"], st["phase"]] = total
        launch(st)

    def reduce_mid(st):
        while st["phase"] < len(plan.phases) - 1:
            reduce_step(st)

    def reduce_end(st):
        reduce_mid(st)
        return collect(st) / plan.counted

    barrier = pltpu.get_barrier_semaphore()
    friends = [plane_peer(o) for o in range(1, inner * m)]
    if "chips" in plan.phases:
        friends = [chip_peer(o) for o in range(1, n * m // 2)] + [core_peer]
        friends += [z_peer(o, 1 - core) for o in range(1, nz)]
    else:
        friends += [z_peer(o, c) for o in range(1, nz) for c in (core, 1 - core)]
    for f in friends:
        pl.semaphore_signal(barrier, inc=1, device_id=f, device_id_type=MESH)

    loads[0].wait()

    def input_sums(at, _):
        v = x_ref[at, :].astype(F32)
        return v, v * v

    src_w[0, 0] = column_sums(*each(rows, 32, input_sums)(width))
    pl.semaphore_wait(barrier, len(friends))
    red = reduce_start(src_w, got_w, 0)

    def stage_columns(value, staged):
        turned = value.T
        if padded != block:
            staged[...] = jnp.zeros_like(staged)
        for i in range(n):
            staged[i // inner, (i % inner) // 2, i % 2, :block, :] = turned[
                i * block : (i + 1) * block, :
            ].astype(BF16)

    def spread_columns(staged, gathered, sem):
        q = z * 2 + core
        lanes = pl.ds(pl.multiple_of(q * rows, rows), rows)
        own = pltpu.make_async_copy(staged.at[z, :, core], gathered.at[:, :, lanes], sem)
        own.start()
        copies = []
        for o in range(nz):
            for c in (core, 1 - core):
                if o == 0 and c is core:
                    continue
                copies.append(
                    push(staged.at[lax.rem(z + o, nz), :, c], gathered.at[:, :, lanes], z_peer(o, c))
                )
        return copies, own

    def place(zz, c, size=rows):
        return pl.ds(pl.multiple_of((zz * 2 + c) * size, size), size)

    long = rows + EXTRA
    own = place(z, core)
    halo = sorted({plan.hz, nz - plan.hz})
    rest = [o for o in range(1, nz) if o not in halo]

    def gather_start(full, size):
        at = full.at[place(z, core, size)]
        over_z = {o: push(at, at, z_peer(o)) for o in halo + rest}
        return over_z, {0: push(at, at, core_peer)}

    def pass_on(full, size, over_z, across, o):
        over_z[o].wait_recv()
        piece = full.at[place(lax.rem(z + nz - o, nz), core, size)]
        across[o] = push(piece, piece, core_peer)

    loads[1].wait()
    loads[2].wait()
    dact = dot_t(cot_ref[...], pw_ref[...])
    dact2[...] = dact
    dact_all[own, :] = dact.astype(BF16)
    reduce_step(red)
    stage_columns(cot_ref[...].astype(F32), cot_t)
    dact_z, dact_c = gather_start(dact_all, rows)
    for c in loads[3:]:
        c.wait()

    mean = reduce_end(red)
    center = mean[0:1]
    rs1 = 1.0 / jnp.sqrt(mean[1:2] - center * center + EPS)
    gain_in, bias_in = gi_ref[...].reshape(1, -1), bi_ref[...].reshape(1, -1)

    def first_gelu(at, _):
        h = (x_ref[at, :].astype(F32) - center) * rs1
        pre = gain_in * h + bias_in
        t = gelu_inner(pre)
        act[at, :] = (0.5 * pre * (1.0 + t)).astype(BF16)
        h1[at, :] = h
        slope1[at, :] = gelu_slope(pre, t)

    each(rows, 16, first_gelu)()

    steps = plan.hz * inner
    up = copy_to(ysend.at[0], before, (lax.rem(me + steps, n), dp))
    down = copy_to(ysend.at[1], after, (lax.rem(me + n - steps, n), dp))
    has_next, has_prev = me < n - steps, me >= steps

    @pl.when(has_next)
    def _():
        ysend[0] = packed(dot(act[...], cw_ref[:, :mid]))
        up.start()

    @pl.when(has_prev)
    def _():
        ysend[1] = packed(dot(act[...], cw_ref[:, 2 * mid :]))
        down.start()

    conv, h2, dpre2 = (mids.at[:, k * mid : (k + 1) * mid] for k in range(3))
    conv[...] = dot(act[...], cw_ref[:, mid : 2 * mid])
    stage_columns(act[...].astype(F32), act_t)

    @pl.when(has_prev)
    def _():
        up.wait_recv()

    @pl.when(jnp.logical_not(has_prev))
    def _():
        before[...] = jnp.zeros_like(before)

    @pl.when(has_next)
    def _():
        down.wait_recv()

    @pl.when(jnp.logical_not(has_next))
    def _():
        after[...] = jnp.zeros_like(after)

    def mean_row(ref, start):
        tail = ref[pl.ds(start, EXTRA), :].astype(F32)
        return tail[0:1] + tail[1:2] + tail[2:3]

    mean_halo = mean_row(before, rows) + mean_row(after, rows)

    def conv_sums(at, _):
        v = conv[at, :] + before[at, :].astype(F32) + after[at, :].astype(F32) + mean_halo
        conv[at, :] = v
        return v, v * v

    src_m[0, 0] = column_sums(*each(rows, 32, conv_sums)(mid))
    red = reduce_start(src_m, got_m, 0)
    conv_all[place(z, core, long), :] = packed(conv[...])
    reduce_step(red)
    for o in halo + rest:
        pass_on(dact_all, rows, dact_z, dact_c, o)
    conv_z, conv_c = gather_start(conv_all, long)
    act_copies, own_act = spread_columns(act_t, act_all, local_sem.at[1])
    mean = reduce_end(red)
    center = mean[0:1]
    rs2 = 1.0 / jnp.sqrt(mean[1:2] - center * center + EPS)
    gain_mid, bias_mid = gm_ref[...].reshape(1, -1), bm_ref[...].reshape(1, -1)

    def mid_gelu(value):
        h = (value - center) * rs2
        pre = gain_mid * h + bias_mid
        t = gelu_inner(pre)
        return h, (0.5 * pre * (1.0 + t)).astype(BF16), gelu_slope(pre, t)

    def own_gelu(at, i):
        h, a, slope = mid_gelu(conv[at, :])
        d = dact2[at, :] * slope
        act2_all[pl.ds(pl.multiple_of((z * 2 + core) * rows + i, 32), 32), :] = a
        h2[at, :] = h
        dpre2[at, :] = d
        return d, d * h

    src_m[1, 0] = column_sums(*each(rows, 32, own_gelu)(mid))
    red = reduce_start(src_m, got_m, 1)

    reduce_step(red)
    out_ref[...] = (x_ref[...].astype(F32) + dot(act2_all[own, :], pw_ref[...])).astype(BF16)
    stores[0].start()
    cot_copies, own_cot = spread_columns(cot_t, cot_all, local_sem.at[0])
    for o in halo + rest:
        pass_on(conv_all, long, conv_z, conv_c, o)

    def remake(o, c, use):
        piece = lax.rem(z + nz - o, nz) * 2 + c
        offset = mean_row(conv_all, pl.multiple_of(piece * long + rows, 16))

        def body(_, i):
            there = pl.ds(pl.multiple_of(piece * rows + i, 32), 32)
            source = pl.ds(pl.multiple_of(piece * long + i, 16), 32)
            h, a, slope = mid_gelu(conv_all[source, :].astype(F32) + offset)
            act2_all[there, :] = a
            use(there, i, h, dact_all[there, :].astype(F32) * slope)

        each(rows, 32, body)()

    def keep(k):
        def use(_, i, h, d):
            at = pl.ds(pl.multiple_of(k * rows + i, 32), 32)
            kept[0, at, :] = h
            kept[1, at, :] = d

        return use

    for k, o in enumerate(halo):
        remake(o, core, keep(k))
    mean2 = reduce_end(red)
    scale2, first2, second2 = gain_mid * rs2, mean2[0:1], mean2[1:2]

    def to_dconv(there, _, h, d):
        dconv_all[there, :] = (scale2 * (d - first2 - h * second2)).astype(BF16)

    def own_dconv(at, i):
        v = (scale2 * (dpre2[at, :] - first2 - h2[at, :] * second2)).astype(BF16)
        dconv_all[pl.ds(pl.multiple_of((z * 2 + core) * rows + i, 32), 32), :] = v
        stacked[at, mid : 2 * mid] = v

    each(rows, 32, own_dconv)()
    for k, o in enumerate(halo):
        piece = lax.rem(z + nz - o, nz) * 2 + core

        def halo_dconv(_, i):
            at = pl.ds(pl.multiple_of(k * rows + i, 32), 32)
            there = pl.ds(pl.multiple_of(piece * rows + i, 32), 32)
            to_dconv(there, i, kept[0, at, :], kept[1, at, :])

        each(rows, 32, halo_dconv)()
    for has, plane, columns in (
        (z + plan.hz < nz, z + plan.hz, slice(0, mid)),
        (z >= plan.hz, z + nz - plan.hz, slice(2 * mid, 3 * mid)),
    ):

        @pl.when(has)
        def _():
            stacked[:, columns] = dconv_all[place(lax.rem(plane, nz), core), :]

        @pl.when(jnp.logical_not(has))
        def _():
            stacked[:, columns] = jnp.zeros((rows, mid), BF16)

    dact1[...] = dot_t(stacked[...], cw_ref[...])

    def first_back(at, _):
        d = dact1[at, :] * slope1[at, :]
        dact1[at, :] = d
        return d, d * h1[at, :]

    src_w[1, 0] = column_sums(*each(rows, 16, first_back)(width))
    red = reduce_start(src_w, got_w, 1)

    group = nx * m
    mine = xi * m + dp

    def send_parts(columns):
        copies = []
        for o in range(1, group):
            to = lax.rem(mine + o, group)
            tx, ty = lax.div(to, m), lax.rem(to, m)
            copies.append(
                push(
                    part.at[tx, :, columns],
                    parts.at[mine, :, columns],
                    (z * inner + tx * 2 + core, ty),
                )
            )
        parts[pl.ds(mine, 1), :, columns] = part[pl.ds(xi, 1), :, columns]
        return copies

    acc[...] = jnp.zeros_like(acc)
    own_act.wait()
    for c in act_copies:
        c.wait_recv()

    def add_plane(o):
        p = lax.rem(z + nz - o, nz)
        span = 2 * rows
        g = dconv_all[pl.ds(pl.multiple_of(p * span, span), span), :]

        def add(tap, q):
            a = act_all[:, :, pl.ds(pl.multiple_of(q * span, span), span)]
            acc[:, tap * mid : (tap + 1) * mid] += dot(a.reshape(nx * padded, span), g)

        add(1, p)

        @pl.when(p >= plan.hz)
        def _():
            add(0, p - plan.hz)

        @pl.when(p + plan.hz < nz)
        def _():
            add(2, p + plan.hz)

    reduce_step(red)
    for o in rest:
        remake(o, core, to_dconv)
    for o in [0] + halo + rest:
        dact_c[o].wait_recv()
        conv_c[o].wait_recv()
        remake(o, 1 - core, to_dconv)
        add_plane(o)
    part[:, :, : 3 * mid] = acc[...].reshape(nx, padded, 3 * mid).astype(BF16)
    reduce_mid(red)
    part_copies = send_parts(pl.ds(0, 3 * mid))
    own_cot.wait()
    for c in cot_copies:
        c.wait_recv()
    for k in range(nx):
        part[k, :, 3 * mid :] = dot(cot_all[k], act2_all[...]).astype(BF16)
    part_copies += send_parts(pl.ds(3 * mid, mid))

    mean = reduce_end(red)
    scale1 = gain_in * rs1

    def last(at, _):
        grad_ref[at, :] = (
            cot_ref[at, :].astype(F32)
            + scale1 * (dact1[at, :] - mean[0:1] - h1[at, :] * mean[1:2])
        ).astype(BF16)

    each(rows, 16, last)()
    stores[1].start()

    for c in part_copies:
        c.wait_recv()
    total = parts[0].astype(F32)
    for k in range(1, group):
        total = total + parts[k].astype(F32)
    convg_ref[...] = total[:block, : 3 * mid]
    projg_ref[...] = total[:block, 3 * mid :]
    stores[2].start()
    stores[3].start()
    for c in stores:
        c.wait()

    for c in pending:
        c.wait_send()

    @pl.when(has_next)
    def _():
        up.wait_send()

    @pl.when(has_prev)
    def _():
        down.wait_send()


def copy_kernel(count, *refs):
    for i in range(count):
        refs[count + i][...] = refs[i][...]


def per_device(inputs, cotangent, conv_weight, proj_weight, gain_in, bias_in, gain_mid, bias_mid):
    samples, places, width = inputs.shape
    mid = proj_weight.shape[0]
    plan = Plan(
        lax.axis_size("seq"), lax.axis_size("dp"), samples, places, width, mid
    )
    rows, nz, nx, padded = plan.rows, plan.nz, plan.nx, plan.padded
    depth = nz * 2 * rows
    hbm = pl.BlockSpec(memory_space=pl.ANY)
    vmem = pl.BlockSpec(memory_space=pltpu.VMEM)
    outs = (
        jax.ShapeDtypeStruct((rows, width), BF16),
        jax.ShapeDtypeStruct((rows, width), BF16),
        jax.ShapeDtypeStruct((plan.block, 3 * mid), F32),
        jax.ShapeDtypeStruct((plan.block, mid), F32),
    )
    phases = len(plan.phases)
    results = pl.pallas_call(
        functools.partial(kernel, plan),
        out_shape=outs,
        in_specs=[hbm] * 8,
        out_specs=(hbm,) * 4,
        scratch_shapes=[
            pltpu.VMEM((rows, width), BF16),
            pltpu.VMEM((rows, width), BF16),
            pltpu.VMEM((width, 3 * mid), BF16),
            pltpu.VMEM((mid, width), BF16),
            pltpu.VMEM((width,), F32),
            pltpu.VMEM((width,), F32),
            pltpu.VMEM((mid,), F32),
            pltpu.VMEM((mid,), F32),
            *[pltpu.VMEM(o.shape, o.dtype) for o in outs],
            pltpu.VMEM((2, phases, 2, width), F32),
            pltpu.VMEM((2, phases, 2, mid), F32),
            pltpu.VMEM((2, plan.slots, 2, width), F32),
            pltpu.VMEM((2, plan.slots, 2, mid), F32),
            pltpu.VMEM((rows, width), BF16),
            pltpu.VMEM((rows, width), F32),
            pltpu.VMEM((rows, width), F32),
            pltpu.VMEM((rows, width), F32),
            pltpu.VMEM((rows, mid), F32),
            pltpu.VMEM((rows + EXTRA, mid), BF16),
            pltpu.VMEM((rows + EXTRA, mid), BF16),
            pltpu.VMEM((2, rows + EXTRA, mid), BF16),
            pltpu.VMEM((rows, width), F32),
            pltpu.VMEM((nz, nx, 2, padded, rows), BF16),
            pltpu.VMEM((nz, nx, 2, padded, rows), BF16),
            pltpu.VMEM((nx, padded, depth), BF16),
            pltpu.VMEM((nx, padded, depth), BF16),
            pltpu.VMEM((depth, mid), BF16),
            pltpu.VMEM((depth, mid), BF16),
            pltpu.VMEM((depth, mid), BF16),
            pltpu.VMEM((nz * 2 * (rows + EXTRA), mid), BF16),
            pltpu.VMEM((nx, padded, 4 * mid), BF16),
            pltpu.VMEM((nx * plan.m, padded, 4 * mid), BF16),
            pltpu.VMEM((nx * padded, 3 * mid), F32),
            pltpu.VMEM((rows, 3 * mid), BF16),
            pltpu.VMEM((2, 2 * rows, mid), F32),
            pltpu.SemaphoreType.DMA((plan.sems,)),
            pltpu.SemaphoreType.DMA((plan.sems,)),
            pltpu.SemaphoreType.DMA((14,)),
        ],
        compiler_params=pltpu.CompilerParams(
            collective_id=0, has_side_effects=True, vmem_limit_bytes=56 * 1024 * 1024
        ),
    )(
        inputs.reshape(rows, width),
        cotangent.reshape(rows, width),
        conv_weight,
        proj_weight,
        gain_in,
        bias_in,
        gain_mid,
        bias_mid,
    )
    block_out, input_grad, conv_grad, proj_grad = pl.pallas_call(
        functools.partial(copy_kernel, len(outs)),
        out_shape=outs,
        in_specs=[vmem] * len(outs),
        out_specs=(vmem,) * len(outs),
        compiler_params=pltpu.CompilerParams(vmem_limit_bytes=56 * 1024 * 1024),
    )(*results)
    shape = (samples, places, width)
    return (block_out.reshape(shape), input_grad.reshape(shape), conv_grad, proj_grad)


def solution(mesh):
    in_specs = (P("dp", "seq", None), P("dp", "seq", None), P(), P(), P(), P(), P(), P())
    out_specs = (P("dp", "seq", None), P("dp", "seq", None), P("seq", None), P("seq", None))
    return jax.shard_map(
        per_device, mesh=mesh, in_specs=in_specs, out_specs=out_specs, check_vma=False
    )
```

```python
import functools
import math

import jax
import jax.numpy as jnp
from jax import lax
from jax.experimental import pallas as pl
from jax.experimental.pallas import tpu as pltpu
from jax.sharding import PartitionSpec as P

DILATION = 1024
EPS = 1e-05
EXTRA = 16
COEFF = math.sqrt(2.0 / math.pi)
MESH = pl.DeviceIdType.MESH
F32, BF16 = jnp.float32, jnp.bfloat16


def gelu_inner(v):
    return jnp.tanh(COEFF * (v + 0.044715 * v * v * v))


def gelu_slope(v, inner):
    return 0.5 * (1.0 + inner) + 0.5 * v * (1.0 - inner * inner) * COEFF * (
        1.0 + 3.0 * 0.044715 * v * v
    )


def dot(a, b):
    return jnp.dot(a, b, preferred_element_type=F32)


def dot_t(a, b):
    return lax.dot_general(a, b, (((1,), (1,)), ((), ())), preferred_element_type=F32)


def column_sums(a, b):
    return jnp.concatenate(
        [jnp.sum(a, axis=0, keepdims=True), jnp.sum(b, axis=0, keepdims=True)], axis=0
    )


def packed(v):
    m = jnp.mean(v, axis=0, keepdims=True)
    high = m.astype(BF16).astype(F32)
    mid = (m - high).astype(BF16).astype(F32)
    low = m - high - mid
    pad = jnp.zeros((EXTRA - 3, v.shape[1]), F32)
    return jnp.concatenate([v - m, high, mid, low, pad], axis=0).astype(BF16)


def unpacked(v):
    f = v.astype(F32)
    r = v.shape[0] - EXTRA
    return f[:r] + (f[r : r + 1] + f[r + 1 : r + 2] + f[r + 2 : r + 3])


def fold(v):
    return jnp.sum(v.reshape(v.shape[0] // 8, 8, v.shape[1]), axis=0)


def each(count, size, body):
    def step(i, carry):
        new = body(pl.ds(pl.multiple_of(i * size, size), size), i * size)
        return tuple(a + fold(b) for a, b in zip(carry, new or ()))

    def run(width=None):
        init = () if width is None else (jnp.zeros((8, width), F32),) * 2
        return lax.fori_loop(0, count // size, step, init)

    return run


class Plan:
    def __init__(self, n, m, samples, places, width, mid):
        self.n, self.m = n, m
        self.rows, self.width, self.mid = samples * places, width, mid
        self.counted = float(samples * places * n * m)
        steps = DILATION // places
        inner = 2
        while inner * inner < n:
            inner *= 2
        self.inner, self.nz, self.nx = inner, n // inner, inner // 2
        assert steps % inner == 0 and n % inner == 0
        self.hz = steps // inner
        assert 0 < self.hz < self.nz
        self.block = width // n
        self.padded = -(-self.block // 16) * 16
        if n * m <= 32:
            self.phases = ("core", "chips")
        else:
            self.phases = ("z", "lo", "dp")
        size = {"core": 2, "chips": n * m // 2, "lo": inner, "dp": m, "z": self.nz}
        self.sizes = [size[p] for p in self.phases]
        self.slots = sum(s - 1 for s in self.sizes)
        q = self.nz * 2 - 1
        self.sems = 4 * self.slots + 4 * q + 2 * (self.nx * m - 1) + 2


def kernel(
    plan,
    x_hbm, cot_hbm, cw_hbm, pw_hbm, gi_hbm, bi_hbm, gm_hbm, bm_hbm,
    out_hbm, grad_hbm, convg_hbm, projg_hbm,
    x_ref, cot_ref, cw_ref, pw_ref, gi_ref, bi_ref, gm_ref, bm_ref,
    out_ref, grad_ref, convg_ref, projg_ref,
    src_w, src_m, got_w, got_m,
    act, h1, slope1, mids, dact2, before, after, ysend, dact1,
    cot_t, act_t, cot_all, act_all, act2_all, dconv_all, dact_all, conv_all, part, parts, acc, stacked, kept,
    send_sem, recv_sem, local_sem,
):
    n, m, nz, nx, inner = plan.n, plan.m, plan.nz, plan.nx, plan.inner
    rows, mid, width, block, padded = plan.rows, plan.mid, plan.width, plan.block, plan.padded
    me, dp = lax.axis_index("seq"), lax.axis_index("dp")
    z, lo = lax.div(me, inner), lax.rem(me, inner)
    xi, core = lax.div(lo, 2), lax.rem(lo, 2)
    loads = [
        pltpu.make_async_copy(a, b, local_sem.at[2 + i])
        for i, (a, b) in enumerate(
            (
                (x_hbm, x_ref), (cot_hbm, cot_ref), (pw_hbm, pw_ref), (gi_hbm, gi_ref),
                (bi_hbm, bi_ref), (cw_hbm, cw_ref), (gm_hbm, gm_ref), (bm_hbm, bm_ref),
            )
        )
    ]
    stores = [
        pltpu.make_async_copy(a, b, local_sem.at[10 + i])
        for i, (a, b) in enumerate(
            (
                (out_ref, out_hbm), (grad_ref, grad_hbm),
                (convg_ref, convg_hbm), (projg_ref, projg_hbm),
            )
        )
    ]
    for c in loads:
        c.start()
    counter = [0]
    pending = []

    def copy_to(src, dst, target):
        k = counter[0]
        counter[0] += 1
        return pltpu.make_async_remote_copy(
            src_ref=src, dst_ref=dst, send_sem=send_sem.at[k], recv_sem=recv_sem.at[k],
            device_id=target, device_id_type=MESH,
        )

    def push(src, dst, target):
        c = copy_to(src, dst, target)
        c.start()
        pending.append(c)
        return c

    def plane_peer(o):
        j = lax.rem(lo * m + dp + o, inner * m)
        return (z * inner + lax.div(j, m), lax.rem(j, m))

    def z_peer(o, c=None):
        c = core if c is None else c
        return (lax.rem(z + o, nz) * inner + xi * 2 + c, dp)

    def chip_peer(o):
        j = lax.rem((z * nx + xi) * m + dp + o, n * m // 2)
        return (lax.div(j, m) * 2 + core, lax.rem(j, m))

    peers = {
        "core": lambda o: core_peer,
        "chips": chip_peer,
        "lo": lambda o: (z * inner + lax.rem(lo + o, inner), dp),
        "dp": lambda o: (me, lax.rem(dp + o, m)),
        "z": z_peer,
    }
    core_peer = (z * inner + xi * 2 + (1 - core), dp)

    def reduce_start(src, got, which):
        state = dict(src=src, got=got, which=which, phase=0, base=0)
        launch(state)
        return state

    def launch(st):
        ph = st["phase"]
        st["copies"] = [
            push(st["src"].at[st["which"], ph], st["got"].at[st["which"], st["base"] + o - 1],
                 peers[plan.phases[ph]](o))
            for o in range(1, plan.sizes[ph])
        ]

    def collect(st):
        ph = st["phase"]
        total = st["src"][st["which"], ph]
        for i, c in enumerate(st["copies"]):
            c.wait_recv()
            total = total + st["got"][st["which"], st["base"] + i]
        st["base"] += plan.sizes[ph] - 1
        st["phase"] += 1
        return total

    def reduce_step(st):
        total = collect(st)
        st["src"][st["which"], st["phase"]] = total
        launch(st)

    def reduce_mid(st):
        while st["phase"] < len(plan.phases) - 1:
            reduce_step(st)

    def reduce_end(st):
        reduce_mid(st)
        return collect(st) / plan.counted

    barrier = pltpu.get_barrier_semaphore()
    friends = [plane_peer(o) for o in range(1, inner * m)]
    if "chips" in plan.phases:
        friends = [chip_peer(o) for o in range(1, n * m // 2)] + [core_peer]
        friends += [z_peer(o, 1 - core) for o in range(1, nz)]
    else:
        friends += [z_peer(o, c) for o in range(1, nz) for c in (core, 1 - core)]
    for f in friends:
        pl.semaphore_signal(barrier, inc=1, device_id=f, device_id_type=MESH)

    loads[0].wait()

    def input_sums(at, _):
        v = x_ref[at, :].astype(F32)
        return v, v * v

    src_w[0, 0] = column_sums(*each(rows, 32, input_sums)(width))
    pl.semaphore_wait(barrier, len(friends))
    red = reduce_start(src_w, got_w, 0)

    def stage_columns(value, staged):
        turned = value.T
        if padded != block:
            staged[...] = jnp.zeros_like(staged)
        for i in range(n):
            staged[i // inner, (i % inner) // 2, i % 2, :block, :] = turned[
                i * block : (i + 1) * block, :
            ].astype(BF16)

    def spread_columns(staged, gathered, sem):
        q = z * 2 + core
        lanes = pl.ds(pl.multiple_of(q * rows, rows), rows)
        own = pltpu.make_async_copy(staged.at[z, :, core], gathered.at[:, :, lanes], sem)
        own.start()
        copies = []
        for o in range(nz):
            for c in (core, 1 - core):
                if o == 0 and c is core:
                    continue
                copies.append(
                    push(staged.at[lax.rem(z + o, nz), :, c], gathered.at[:, :, lanes], z_peer(o, c))
                )
        return copies, own

    def place(zz, c, size=rows):
        return pl.ds(pl.multiple_of((zz * 2 + c) * size, size), size)

    long = rows + EXTRA
    own = place(z, core)
    halo = sorted({plan.hz, nz - plan.hz})
    rest = [o for o in range(1, nz) if o not in halo]

    relay = nz == 4 and plan.hz == 2
    beside = z + 1 - 2 * lax.rem(z, 2)

    def plane_of(o):
        if relay and o in (1, 3):
            return lax.rem(beside + o - 1, nz)
        return lax.rem(z + nz - o, nz)

    def to_beside(full, size, plane):
        at = full.at[place(plane, core, size)]
        return push(at, at, (beside * inner + xi * 2 + core, dp))

    def gather_start(full, size):
        at = full.at[place(z, core, size)]
        if relay:
            over_z = {2: push(at, at, z_peer(2)), 1: to_beside(full, size, z)}
        else:
            over_z = {o: push(at, at, z_peer(o)) for o in halo + rest}
        return over_z, {0: push(at, at, core_peer)}

    def pass_on(full, size, over_z, across, o):
        over_z[o].wait_recv()
        if relay and o == 2:
            over_z[3] = to_beside(full, size, plane_of(2))
        piece = full.at[place(plane_of(o), core, size)]
        across[o] = push(piece, piece, core_peer)

    loads[1].wait()
    loads[2].wait()
    dact = dot_t(cot_ref[...], pw_ref[...])
    dact2[...] = dact
    dact_all[own, :] = dact.astype(BF16)
    reduce_step(red)
    stage_columns(cot_ref[...].astype(F32), cot_t)
    dact_z, dact_c = gather_start(dact_all, rows)
    for c in loads[3:]:
        c.wait()

    mean = reduce_end(red)
    center = mean[0:1]
    rs1 = 1.0 / jnp.sqrt(mean[1:2] - center * center + EPS)
    gain_in, bias_in = gi_ref[...].reshape(1, -1), bi_ref[...].reshape(1, -1)

    def first_gelu(at, _):
        h = (x_ref[at, :].astype(F32) - center) * rs1
        pre = gain_in * h + bias_in
        t = gelu_inner(pre)
        act[at, :] = (0.5 * pre * (1.0 + t)).astype(BF16)
        h1[at, :] = h
        slope1[at, :] = gelu_slope(pre, t)

    each(rows, 16, first_gelu)()

    steps = plan.hz * inner
    up = copy_to(ysend.at[0], before, (lax.rem(me + steps, n), dp))
    down = copy_to(ysend.at[1], after, (lax.rem(me + n - steps, n), dp))
    has_next, has_prev = me < n - steps, me >= steps

    @pl.when(has_next)
    def _():
        ysend[0] = packed(dot(act[...], cw_ref[:, :mid]))
        up.start()

    @pl.when(has_prev)
    def _():
        ysend[1] = packed(dot(act[...], cw_ref[:, 2 * mid :]))
        down.start()

    conv, h2, dpre2 = (mids.at[:, k * mid : (k + 1) * mid] for k in range(3))
    conv[...] = dot(act[...], cw_ref[:, mid : 2 * mid])
    stage_columns(act[...].astype(F32), act_t)

    @pl.when(has_prev)
    def _():
        up.wait_recv()

    @pl.when(jnp.logical_not(has_prev))
    def _():
        before[...] = jnp.zeros_like(before)

    @pl.when(has_next)
    def _():
        down.wait_recv()

    @pl.when(jnp.logical_not(has_next))
    def _():
        after[...] = jnp.zeros_like(after)

    def mean_row(ref, start):
        tail = ref[pl.ds(start, EXTRA), :].astype(F32)
        return tail[0:1] + tail[1:2] + tail[2:3]

    mean_halo = mean_row(before, rows) + mean_row(after, rows)

    def conv_sums(at, _):
        v = conv[at, :] + before[at, :].astype(F32) + after[at, :].astype(F32) + mean_halo
        conv[at, :] = v
        return v, v * v

    src_m[0, 0] = column_sums(*each(rows, 32, conv_sums)(mid))
    red = reduce_start(src_m, got_m, 0)
    conv_all[place(z, core, long), :] = packed(conv[...])
    reduce_step(red)
    for o in halo + rest[:-1]:
        pass_on(dact_all, rows, dact_z, dact_c, o)
    conv_z, conv_c = gather_start(conv_all, long)
    act_copies, own_act = spread_columns(act_t, act_all, local_sem.at[1])
    mean = reduce_end(red)
    center = mean[0:1]
    rs2 = 1.0 / jnp.sqrt(mean[1:2] - center * center + EPS)
    gain_mid, bias_mid = gm_ref[...].reshape(1, -1), bm_ref[...].reshape(1, -1)

    def mid_gelu(value):
        h = (value - center) * rs2
        pre = gain_mid * h + bias_mid
        t = gelu_inner(pre)
        return h, (0.5 * pre * (1.0 + t)).astype(BF16), gelu_slope(pre, t)

    def own_gelu(at, i):
        h, a, slope = mid_gelu(conv[at, :])
        d = dact2[at, :] * slope
        act2_all[pl.ds(pl.multiple_of((z * 2 + core) * rows + i, 32), 32), :] = a
        h2[at, :] = h
        dpre2[at, :] = d
        return d, d * h

    src_m[1, 0] = column_sums(*each(rows, 32, own_gelu)(mid))
    red = reduce_start(src_m, got_m, 1)

    reduce_step(red)
    out_ref[...] = (x_ref[...].astype(F32) + dot(act2_all[own, :], pw_ref[...])).astype(BF16)
    stores[0].start()
    cot_copies, own_cot = spread_columns(cot_t, cot_all, local_sem.at[0])
    for o in halo + rest:
        if o != rest[-1]:
            pass_on(conv_all, long, conv_z, conv_c, o)

    def remake(o, c, use):
        piece = plane_of(o) * 2 + c
        offset = mean_row(conv_all, pl.multiple_of(piece * long + rows, 16))

        def body(_, i):
            there = pl.ds(pl.multiple_of(piece * rows + i, 32), 32)
            source = pl.ds(pl.multiple_of(piece * long + i, 16), 32)
            h, a, slope = mid_gelu(conv_all[source, :].astype(F32) + offset)
            act2_all[there, :] = a
            use(there, i, h, dact_all[there, :].astype(F32) * slope)

        each(rows, 32, body)()

    def keep(k):
        def use(_, i, h, d):
            at = pl.ds(pl.multiple_of(k * rows + i, 32), 32)
            kept[0, at, :] = h
            kept[1, at, :] = d

        return use

    for k, o in enumerate(halo):
        remake(o, core, keep(k))
    mean2 = reduce_end(red)
    scale2, first2, second2 = gain_mid * rs2, mean2[0:1], mean2[1:2]

    def to_dconv(there, _, h, d):
        dconv_all[there, :] = (scale2 * (d - first2 - h * second2)).astype(BF16)

    def own_dconv(at, i):
        v = (scale2 * (dpre2[at, :] - first2 - h2[at, :] * second2)).astype(BF16)
        dconv_all[pl.ds(pl.multiple_of((z * 2 + core) * rows + i, 32), 32), :] = v
        stacked[at, mid : 2 * mid] = v

    each(rows, 32, own_dconv)()
    for k, o in enumerate(halo):
        piece = plane_of(o) * 2 + core

        def halo_dconv(_, i):
            at = pl.ds(pl.multiple_of(k * rows + i, 32), 32)
            there = pl.ds(pl.multiple_of(piece * rows + i, 32), 32)
            to_dconv(there, i, kept[0, at, :], kept[1, at, :])

        each(rows, 32, halo_dconv)()
    for has, plane, columns in (
        (z + plan.hz < nz, z + plan.hz, slice(0, mid)),
        (z >= plan.hz, z + nz - plan.hz, slice(2 * mid, 3 * mid)),
    ):

        @pl.when(has)
        def _():
            stacked[:, columns] = dconv_all[place(lax.rem(plane, nz), core), :]

        @pl.when(jnp.logical_not(has))
        def _():
            stacked[:, columns] = jnp.zeros((rows, mid), BF16)

    dact1[...] = dot_t(stacked[...], cw_ref[...])

    def first_back(at, _):
        d = dact1[at, :] * slope1[at, :]
        dact1[at, :] = d
        return d, d * h1[at, :]

    src_w[1, 0] = column_sums(*each(rows, 16, first_back)(width))
    red = reduce_start(src_w, got_w, 1)

    group = nx * m
    mine = xi * m + dp

    def send_parts(columns):
        copies = []
        for o in range(1, group):
            to = lax.rem(mine + o, group)
            tx, ty = lax.div(to, m), lax.rem(to, m)
            copies.append(
                push(
                    part.at[tx, :, columns],
                    parts.at[mine, :, columns],
                    (z * inner + tx * 2 + core, ty),
                )
            )
        parts[pl.ds(mine, 1), :, columns] = part[pl.ds(xi, 1), :, columns]
        return copies

    acc[...] = jnp.zeros_like(acc)
    own_act.wait()
    for c in act_copies:
        c.wait_recv()

    def add_plane(o):
        p = plane_of(o)
        span = 2 * rows
        g = dconv_all[pl.ds(pl.multiple_of(p * span, span), span), :]

        def add(tap, q):
            a = act_all[:, :, pl.ds(pl.multiple_of(q * span, span), span)]
            acc[:, tap * mid : (tap + 1) * mid] += dot(a.reshape(nx * padded, span), g)

        add(1, p)

        @pl.when(p >= plan.hz)
        def _():
            add(0, p - plan.hz)

        @pl.when(p + plan.hz < nz)
        def _():
            add(2, p + plan.hz)

    reduce_step(red)
    pass_on(dact_all, rows, dact_z, dact_c, rest[-1])
    pass_on(conv_all, long, conv_z, conv_c, rest[-1])
    for o in rest:
        remake(o, core, to_dconv)
    for o in [0] + halo + rest:
        dact_c[o].wait_recv()
        conv_c[o].wait_recv()
        remake(o, 1 - core, to_dconv)
        add_plane(o)
    part[:, :, : 3 * mid] = acc[...].reshape(nx, padded, 3 * mid).astype(BF16)
    reduce_mid(red)
    part_copies = send_parts(pl.ds(0, 3 * mid))
    own_cot.wait()
    for c in cot_copies:
        c.wait_recv()
    for k in range(nx):
        part[k, :, 3 * mid :] = dot(cot_all[k], act2_all[...]).astype(BF16)
    part_copies += send_parts(pl.ds(3 * mid, mid))

    mean = reduce_end(red)
    scale1 = gain_in * rs1

    def last(at, _):
        grad_ref[at, :] = (
            cot_ref[at, :].astype(F32)
            + scale1 * (dact1[at, :] - mean[0:1] - h1[at, :] * mean[1:2])
        ).astype(BF16)

    each(rows, 16, last)()
    stores[1].start()

    for c in part_copies:
        c.wait_recv()
    total = parts[0].astype(F32)
    for k in range(1, group):
        total = total + parts[k].astype(F32)
    convg_ref[...] = total[:block, : 3 * mid]
    projg_ref[...] = total[:block, 3 * mid :]
    stores[2].start()
    stores[3].start()
    for c in stores:
        c.wait()

    for c in pending:
        c.wait_send()

    @pl.when(has_next)
    def _():
        up.wait_send()

    @pl.when(has_prev)
    def _():
        down.wait_send()


def copy_kernel(count, *refs):
    for i in range(count):
        refs[count + i][...] = refs[i][...]


def per_device(inputs, cotangent, conv_weight, proj_weight, gain_in, bias_in, gain_mid, bias_mid):
    samples, places, width = inputs.shape
    mid = proj_weight.shape[0]
    plan = Plan(
        lax.axis_size("seq"), lax.axis_size("dp"), samples, places, width, mid
    )
    rows, nz, nx, padded = plan.rows, plan.nz, plan.nx, plan.padded
    depth = nz * 2 * rows
    hbm = pl.BlockSpec(memory_space=pl.ANY)
    vmem = pl.BlockSpec(memory_space=pltpu.VMEM)
    outs = (
        jax.ShapeDtypeStruct((rows, width), BF16),
        jax.ShapeDtypeStruct((rows, width), BF16),
        jax.ShapeDtypeStruct((plan.block, 3 * mid), F32),
        jax.ShapeDtypeStruct((plan.block, mid), F32),
    )
    phases = len(plan.phases)
    results = pl.pallas_call(
        functools.partial(kernel, plan),
        out_shape=outs,
        in_specs=[hbm] * 8,
        out_specs=(hbm,) * 4,
        scratch_shapes=[
            pltpu.VMEM((rows, width), BF16),
            pltpu.VMEM((rows, width), BF16),
            pltpu.VMEM((width, 3 * mid), BF16),
            pltpu.VMEM((mid, width), BF16),
            pltpu.VMEM((width,), F32),
            pltpu.VMEM((width,), F32),
            pltpu.VMEM((mid,), F32),
            pltpu.VMEM((mid,), F32),
            *[pltpu.VMEM(o.shape, o.dtype) for o in outs],
            pltpu.VMEM((2, phases, 2, width), F32),
            pltpu.VMEM((2, phases, 2, mid), F32),
            pltpu.VMEM((2, plan.slots, 2, width), F32),
            pltpu.VMEM((2, plan.slots, 2, mid), F32),
            pltpu.VMEM((rows, width), BF16),
            pltpu.VMEM((rows, width), F32),
            pltpu.VMEM((rows, width), F32),
            pltpu.VMEM((rows, width), F32),
            pltpu.VMEM((rows, mid), F32),
            pltpu.VMEM((rows + EXTRA, mid), BF16),
            pltpu.VMEM((rows + EXTRA, mid), BF16),
            pltpu.VMEM((2, rows + EXTRA, mid), BF16),
            pltpu.VMEM((rows, width), F32),
            pltpu.VMEM((nz, nx, 2, padded, rows), BF16),
            pltpu.VMEM((nz, nx, 2, padded, rows), BF16),
            pltpu.VMEM((nx, padded, depth), BF16),
            pltpu.VMEM((nx, padded, depth), BF16),
            pltpu.VMEM((depth, mid), BF16),
            pltpu.VMEM((depth, mid), BF16),
            pltpu.VMEM((depth, mid), BF16),
            pltpu.VMEM((nz * 2 * (rows + EXTRA), mid), BF16),
            pltpu.VMEM((nx, padded, 4 * mid), BF16),
            pltpu.VMEM((nx * plan.m, padded, 4 * mid), BF16),
            pltpu.VMEM((nx * padded, 3 * mid), F32),
            pltpu.VMEM((rows, 3 * mid), BF16),
            pltpu.VMEM((2, 2 * rows, mid), F32),
            pltpu.SemaphoreType.DMA((plan.sems,)),
            pltpu.SemaphoreType.DMA((plan.sems,)),
            pltpu.SemaphoreType.DMA((14,)),
        ],
        compiler_params=pltpu.CompilerParams(
            collective_id=0, has_side_effects=True, vmem_limit_bytes=56 * 1024 * 1024
        ),
    )(
        inputs.reshape(rows, width),
        cotangent.reshape(rows, width),
        conv_weight,
        proj_weight,
        gain_in,
        bias_in,
        gain_mid,
        bias_mid,
    )
    block_out, input_grad, conv_grad, proj_grad = pl.pallas_call(
        functools.partial(copy_kernel, len(outs)),
        out_shape=outs,
        in_specs=[vmem] * len(outs),
        out_specs=(vmem,) * len(outs),
        compiler_params=pltpu.CompilerParams(vmem_limit_bytes=56 * 1024 * 1024),
    )(*results)
    shape = (samples, places, width)
    return (block_out.reshape(shape), input_grad.reshape(shape), conv_grad, proj_grad)


def solution(mesh):
    in_specs = (P("dp", "seq", None), P("dp", "seq", None), P(), P(), P(), P(), P(), P())
    out_specs = (P("dp", "seq", None), P("dp", "seq", None), P("seq", None), P("seq", None))
    return jax.shard_map(
        per_device, mesh=mesh, in_specs=in_specs, out_specs=out_specs, check_vma=False
    )
```

```python
import functools
import math

import jax
import jax.numpy as jnp
from jax import lax
from jax.experimental import pallas as pl
from jax.experimental.pallas import tpu as pltpu
from jax.sharding import PartitionSpec as P

DILATION = 1024
EPS = 1e-05
EXTRA = 16
COEFF = math.sqrt(2.0 / math.pi)
MESH = pl.DeviceIdType.MESH
F32, BF16 = jnp.float32, jnp.bfloat16


def gelu_inner(v):
    return jnp.tanh(COEFF * (v + 0.044715 * v * v * v))


def gelu_slope(v, inner):
    return 0.5 * (1.0 + inner) + 0.5 * v * (1.0 - inner * inner) * COEFF * (
        1.0 + 3.0 * 0.044715 * v * v
    )


def dot(a, b):
    return jnp.dot(a, b, preferred_element_type=F32)


def dot_t(a, b):
    return lax.dot_general(a, b, (((1,), (1,)), ((), ())), preferred_element_type=F32)


def column_sums(a, b):
    return jnp.concatenate(
        [jnp.sum(a, axis=0, keepdims=True), jnp.sum(b, axis=0, keepdims=True)], axis=0
    )


def packed(v):
    m = jnp.mean(v, axis=0, keepdims=True)
    high = m.astype(BF16).astype(F32)
    mid = (m - high).astype(BF16).astype(F32)
    low = m - high - mid
    pad = jnp.zeros((EXTRA - 3, v.shape[1]), F32)
    return jnp.concatenate([v - m, high, mid, low, pad], axis=0).astype(BF16)


def unpacked(v):
    f = v.astype(F32)
    r = v.shape[0] - EXTRA
    return f[:r] + (f[r : r + 1] + f[r + 1 : r + 2] + f[r + 2 : r + 3])


def fold(v):
    return jnp.sum(v.reshape(v.shape[0] // 8, 8, v.shape[1]), axis=0)


def each(count, size, body):
    def step(i, carry):
        new = body(pl.ds(pl.multiple_of(i * size, size), size), i * size)
        return tuple(a + fold(b) for a, b in zip(carry, new or ()))

    def run(width=None):
        init = () if width is None else (jnp.zeros((8, width), F32),) * 2
        return lax.fori_loop(0, count // size, step, init)

    return run


class Plan:
    def __init__(self, n, m, samples, places, width, mid):
        self.n, self.m = n, m
        self.rows, self.width, self.mid = samples * places, width, mid
        self.counted = float(samples * places * n * m)
        steps = DILATION // places
        inner = 2
        while inner * inner < n:
            inner *= 2
        self.inner, self.nz, self.nx = inner, n // inner, inner // 2
        assert steps % inner == 0 and n % inner == 0
        self.hz = steps // inner
        assert 0 < self.hz < self.nz
        self.block = width // n
        self.padded = -(-self.block // 16) * 16
        if n * m <= 32:
            self.phases = ("core", "chips")
        else:
            self.phases = ("z", "lo", "dp")
        size = {"core": 2, "chips": n * m // 2, "lo": inner, "dp": m, "z": self.nz}
        self.sizes = [size[p] for p in self.phases]
        self.slots = sum(s - 1 for s in self.sizes)
        q = self.nz * 2 - 1
        self.sems = 4 * self.slots + 4 * q + 2 * (self.nx * m - 1) + 2


def kernel(
    plan,
    x_hbm, cot_hbm, cw_hbm, pw_hbm, gi_hbm, bi_hbm, gm_hbm, bm_hbm,
    out_hbm, grad_hbm, convg_hbm, projg_hbm,
    x_ref, cot_ref, cw_ref, pw_ref, gi_ref, bi_ref, gm_ref, bm_ref,
    out_ref, grad_ref, convg_ref, projg_ref,
    src_w, src_m, got_w, got_m,
    act, h1, slope1, mids, dact2, before, after, ysend, dact1,
    cot_t, act_t, cot_all, act_all, act2_all, dconv_all, dact_all, conv_all, part, parts, acc, stacked, kept,
    send_sem, recv_sem, local_sem,
):
    n, m, nz, nx, inner = plan.n, plan.m, plan.nz, plan.nx, plan.inner
    rows, mid, width, block, padded = plan.rows, plan.mid, plan.width, plan.block, plan.padded
    me, dp = lax.axis_index("seq"), lax.axis_index("dp")
    z, lo = lax.div(me, inner), lax.rem(me, inner)
    xi, core = lax.div(lo, 2), lax.rem(lo, 2)
    loads = [
        pltpu.make_async_copy(a, b, local_sem.at[2 + i])
        for i, (a, b) in enumerate(
            (
                (x_hbm, x_ref), (cot_hbm, cot_ref), (pw_hbm, pw_ref), (gi_hbm, gi_ref),
                (bi_hbm, bi_ref), (cw_hbm, cw_ref), (gm_hbm, gm_ref), (bm_hbm, bm_ref),
            )
        )
    ]
    stores = [
        pltpu.make_async_copy(a, b, local_sem.at[10 + i])
        for i, (a, b) in enumerate(
            (
                (out_ref, out_hbm), (grad_ref, grad_hbm),
                (convg_ref, convg_hbm), (projg_ref, projg_hbm),
            )
        )
    ]
    for c in loads:
        c.start()
    counter = [0]
    pending = []

    def copy_to(src, dst, target):
        k = counter[0]
        counter[0] += 1
        return pltpu.make_async_remote_copy(
            src_ref=src, dst_ref=dst, send_sem=send_sem.at[k], recv_sem=recv_sem.at[k],
            device_id=target, device_id_type=MESH,
        )

    def push(src, dst, target):
        c = copy_to(src, dst, target)
        c.start()
        pending.append(c)
        return c

    def plane_peer(o):
        j = lax.rem(lo * m + dp + o, inner * m)
        return (z * inner + lax.div(j, m), lax.rem(j, m))

    def z_peer(o, c=None):
        c = core if c is None else c
        return (lax.rem(z + o, nz) * inner + xi * 2 + c, dp)

    def chip_peer(o):
        j = lax.rem((z * nx + xi) * m + dp + o, n * m // 2)
        return (lax.div(j, m) * 2 + core, lax.rem(j, m))

    peers = {
        "core": lambda o: core_peer,
        "chips": chip_peer,
        "lo": lambda o: (z * inner + lax.rem(lo + o, inner), dp),
        "dp": lambda o: (me, lax.rem(dp + o, m)),
        "z": z_peer,
    }
    core_peer = (z * inner + xi * 2 + (1 - core), dp)

    def reduce_start(src, got, which):
        state = dict(src=src, got=got, which=which, phase=0, base=0)
        launch(state)
        return state

    def launch(st):
        ph = st["phase"]
        st["copies"] = [
            push(st["src"].at[st["which"], ph], st["got"].at[st["which"], st["base"] + o - 1],
                 peers[plan.phases[ph]](o))
            for o in range(1, plan.sizes[ph])
        ]

    def collect(st):
        ph = st["phase"]
        total = st["src"][st["which"], ph]
        for i, c in enumerate(st["copies"]):
            c.wait_recv()
            total = total + st["got"][st["which"], st["base"] + i]
        st["base"] += plan.sizes[ph] - 1
        st["phase"] += 1
        return total

    def reduce_step(st):
        total = collect(st)
        st["src"][st["which"], st["phase"]] = total
        launch(st)

    def reduce_mid(st):
        while st["phase"] < len(plan.phases) - 1:
            reduce_step(st)

    def reduce_end(st):
        reduce_mid(st)
        return collect(st) / plan.counted

    barrier = pltpu.get_barrier_semaphore()
    friends = [plane_peer(o) for o in range(1, inner * m)]
    if "chips" in plan.phases:
        friends = [chip_peer(o) for o in range(1, n * m // 2)] + [core_peer]
        friends += [z_peer(o, 1 - core) for o in range(1, nz)]
    else:
        friends += [z_peer(o, c) for o in range(1, nz) for c in (core, 1 - core)]
    for f in friends:
        pl.semaphore_signal(barrier, inc=1, device_id=f, device_id_type=MESH)

    loads[0].wait()

    def input_sums(at, _):
        v = x_ref[at, :].astype(F32)
        return v, v * v

    src_w[0, 0] = column_sums(*each(rows, 32, input_sums)(width))
    pl.semaphore_wait(barrier, len(friends))
    red = reduce_start(src_w, got_w, 0)

    def stage_columns(value, staged):
        turned = value.T
        if padded != block:
            staged[...] = jnp.zeros_like(staged)
        for i in range(n):
            staged[i // inner, (i % inner) // 2, i % 2, :block, :] = turned[
                i * block : (i + 1) * block, :
            ].astype(BF16)

    def spread_columns(staged, gathered, sem):
        q = z * 2 + core
        lanes = pl.ds(pl.multiple_of(q * rows, rows), rows)
        own = pltpu.make_async_copy(staged.at[z, :, core], gathered.at[:, :, lanes], sem)
        own.start()
        copies = []
        for o in range(nz):
            for c in (core, 1 - core):
                if o == 0 and c is core:
                    continue
                copies.append(
                    push(staged.at[lax.rem(z + o, nz), :, c], gathered.at[:, :, lanes], z_peer(o, c))
                )
        return copies, own

    def place(zz, c, size=rows):
        return pl.ds(pl.multiple_of((zz * 2 + c) * size, size), size)

    long = rows + EXTRA
    own = place(z, core)
    halo = sorted({plan.hz, nz - plan.hz})
    rest = [o for o in range(1, nz) if o not in halo]

    relay = nz == 4 and plan.hz == 2
    beside = z + 1 - 2 * lax.rem(z, 2)

    def plane_of(o):
        if relay and o in (1, 3):
            return lax.rem(beside + o - 1, nz)
        return lax.rem(z + nz - o, nz)

    def to_beside(full, size, plane):
        at = full.at[place(plane, core, size)]
        return push(at, at, (beside * inner + xi * 2 + core, dp))

    def gather_start(full, size):
        at = full.at[place(z, core, size)]
        if relay:
            over_z = {2: push(at, at, z_peer(2)), 1: to_beside(full, size, z)}
        else:
            over_z = {o: push(at, at, z_peer(o)) for o in halo + rest}
        return over_z, {0: push(at, at, core_peer)}

    def pass_on(full, size, over_z, across, o):
        over_z[o].wait_recv()
        if relay and o == 2:
            over_z[3] = to_beside(full, size, plane_of(2))
        piece = full.at[place(plane_of(o), core, size)]
        across[o] = push(piece, piece, core_peer)

    loads[1].wait()
    loads[2].wait()
    dact = dot_t(cot_ref[...], pw_ref[...])
    dact2[...] = dact
    dact_all[own, :] = dact.astype(BF16)
    reduce_step(red)
    stage_columns(cot_ref[...].astype(F32), cot_t)
    dact_z, dact_c = gather_start(dact_all, rows)
    for c in loads[3:]:
        c.wait()

    mean = reduce_end(red)
    center = mean[0:1]
    rs1 = 1.0 / jnp.sqrt(mean[1:2] - center * center + EPS)
    gain_in, bias_in = gi_ref[...].reshape(1, -1), bi_ref[...].reshape(1, -1)

    def first_gelu(at, _):
        h = (x_ref[at, :].astype(F32) - center) * rs1
        pre = gain_in * h + bias_in
        t = gelu_inner(pre)
        act[at, :] = (0.5 * pre * (1.0 + t)).astype(BF16)
        h1[at, :] = h
        slope1[at, :] = gelu_slope(pre, t)

    each(rows, 16, first_gelu)()

    steps = plan.hz * inner
    up = copy_to(ysend.at[0], before, (lax.rem(me + steps, n), dp))
    down = copy_to(ysend.at[1], after, (lax.rem(me + n - steps, n), dp))
    has_next, has_prev = me < n - steps, me >= steps

    @pl.when(has_next)
    def _():
        ysend[0] = packed(dot(act[...], cw_ref[:, :mid]))
        up.start()

    @pl.when(has_prev)
    def _():
        ysend[1] = packed(dot(act[...], cw_ref[:, 2 * mid :]))
        down.start()

    conv, h2, dpre2 = (mids.at[:, k * mid : (k + 1) * mid] for k in range(3))
    conv[...] = dot(act[...], cw_ref[:, mid : 2 * mid])
    stage_columns(act[...].astype(F32), act_t)

    @pl.when(has_prev)
    def _():
        up.wait_recv()

    @pl.when(jnp.logical_not(has_prev))
    def _():
        before[...] = jnp.zeros_like(before)

    @pl.when(has_next)
    def _():
        down.wait_recv()

    @pl.when(jnp.logical_not(has_next))
    def _():
        after[...] = jnp.zeros_like(after)

    def mean_row(ref, start):
        tail = ref[pl.ds(start, EXTRA), :].astype(F32)
        return tail[0:1] + tail[1:2] + tail[2:3]

    mean_halo = mean_row(before, rows) + mean_row(after, rows)

    def conv_sums(at, _):
        v = conv[at, :] + before[at, :].astype(F32) + after[at, :].astype(F32) + mean_halo
        conv[at, :] = v
        return v, v * v

    src_m[0, 0] = column_sums(*each(rows, 32, conv_sums)(mid))
    red = reduce_start(src_m, got_m, 0)
    conv_all[place(z, core, long), :] = packed(conv[...])
    reduce_step(red)
    for o in halo + rest[:-1]:
        pass_on(dact_all, rows, dact_z, dact_c, o)
    conv_z, conv_c = gather_start(conv_all, long)
    act_copies, own_act = spread_columns(act_t, act_all, local_sem.at[1])
    mean = reduce_end(red)
    center = mean[0:1]
    rs2 = 1.0 / jnp.sqrt(mean[1:2] - center * center + EPS)
    gain_mid, bias_mid = gm_ref[...].reshape(1, -1), bm_ref[...].reshape(1, -1)

    def mid_gelu(value):
        h = (value - center) * rs2
        pre = gain_mid * h + bias_mid
        t = gelu_inner(pre)
        return h, (0.5 * pre * (1.0 + t)).astype(BF16), gelu_slope(pre, t)

    def own_gelu(at, i):
        h, a, slope = mid_gelu(conv[at, :])
        d = dact2[at, :] * slope
        act2_all[pl.ds(pl.multiple_of((z * 2 + core) * rows + i, 32), 32), :] = a
        h2[at, :] = h
        dpre2[at, :] = d
        return d, d * h

    src_m[1, 0] = column_sums(*each(rows, 32, own_gelu)(mid))
    red = reduce_start(src_m, got_m, 1)

    reduce_step(red)
    out_ref[...] = (x_ref[...].astype(F32) + dot(act2_all[own, :], pw_ref[...])).astype(BF16)
    stores[0].start()
    for o in halo + rest:
        if o != rest[-1]:
            pass_on(conv_all, long, conv_z, conv_c, o)

    def remake(o, c, use):
        piece = plane_of(o) * 2 + c
        offset = mean_row(conv_all, pl.multiple_of(piece * long + rows, 16))

        def body(_, i):
            there = pl.ds(pl.multiple_of(piece * rows + i, 32), 32)
            source = pl.ds(pl.multiple_of(piece * long + i, 16), 32)
            h, a, slope = mid_gelu(conv_all[source, :].astype(F32) + offset)
            act2_all[there, :] = a
            use(there, i, h, dact_all[there, :].astype(F32) * slope)

        each(rows, 32, body)()

    def keep(k):
        def use(_, i, h, d):
            at = pl.ds(pl.multiple_of(k * rows + i, 32), 32)
            kept[0, at, :] = h
            kept[1, at, :] = d

        return use

    cot_copies, own_cot = spread_columns(cot_t, cot_all, local_sem.at[0])
    for k, o in enumerate(halo):
        remake(o, core, keep(k))
    mean2 = reduce_end(red)
    scale2, first2, second2 = gain_mid * rs2, mean2[0:1], mean2[1:2]

    def to_dconv(there, _, h, d):
        dconv_all[there, :] = (scale2 * (d - first2 - h * second2)).astype(BF16)

    def own_dconv(at, i):
        v = (scale2 * (dpre2[at, :] - first2 - h2[at, :] * second2)).astype(BF16)
        dconv_all[pl.ds(pl.multiple_of((z * 2 + core) * rows + i, 32), 32), :] = v
        stacked[at, mid : 2 * mid] = v

    each(rows, 32, own_dconv)()
    for k, o in enumerate(halo):
        piece = plane_of(o) * 2 + core

        def halo_dconv(_, i):
            at = pl.ds(pl.multiple_of(k * rows + i, 32), 32)
            there = pl.ds(pl.multiple_of(piece * rows + i, 32), 32)
            to_dconv(there, i, kept[0, at, :], kept[1, at, :])

        each(rows, 32, halo_dconv)()
    for has, plane, columns in (
        (z + plan.hz < nz, z + plan.hz, slice(0, mid)),
        (z >= plan.hz, z + nz - plan.hz, slice(2 * mid, 3 * mid)),
    ):

        @pl.when(has)
        def _():
            stacked[:, columns] = dconv_all[place(lax.rem(plane, nz), core), :]

        @pl.when(jnp.logical_not(has))
        def _():
            stacked[:, columns] = jnp.zeros((rows, mid), BF16)

    dact1[...] = dot_t(stacked[...], cw_ref[...])

    def first_back(at, _):
        d = dact1[at, :] * slope1[at, :]
        dact1[at, :] = d
        return d, d * h1[at, :]

    src_w[1, 0] = column_sums(*each(rows, 16, first_back)(width))
    red = reduce_start(src_w, got_w, 1)

    group = nx * m
    mine = xi * m + dp

    def send_parts(columns):
        copies = []
        for o in range(1, group):
            to = lax.rem(mine + o, group)
            tx, ty = lax.div(to, m), lax.rem(to, m)
            copies.append(
                push(
                    part.at[tx, :, columns],
                    parts.at[mine, :, columns],
                    (z * inner + tx * 2 + core, ty),
                )
            )
        parts[pl.ds(mine, 1), :, columns] = part[pl.ds(xi, 1), :, columns]
        return copies

    acc[...] = jnp.zeros_like(acc)
    own_act.wait()
    for c in act_copies:
        c.wait_recv()

    def add_plane(o):
        p = plane_of(o)
        span = 2 * rows
        g = dconv_all[pl.ds(pl.multiple_of(p * span, span), span), :]

        def add(tap, q):
            a = act_all[:, :, pl.ds(pl.multiple_of(q * span, span), span)]
            acc[:, tap * mid : (tap + 1) * mid] += dot(a.reshape(nx * padded, span), g)

        add(1, p)

        @pl.when(p >= plan.hz)
        def _():
            add(0, p - plan.hz)

        @pl.when(p + plan.hz < nz)
        def _():
            add(2, p + plan.hz)

    reduce_step(red)
    pass_on(dact_all, rows, dact_z, dact_c, rest[-1])
    pass_on(conv_all, long, conv_z, conv_c, rest[-1])
    for o in rest:
        remake(o, core, to_dconv)
    for o in [0] + halo + rest:
        dact_c[o].wait_recv()
        conv_c[o].wait_recv()
        remake(o, 1 - core, to_dconv)
        add_plane(o)
    part[:, :, : 3 * mid] = acc[...].reshape(nx, padded, 3 * mid).astype(BF16)
    reduce_mid(red)
    part_copies = send_parts(pl.ds(0, 3 * mid))
    own_cot.wait()
    for c in cot_copies:
        c.wait_recv()
    for k in range(nx):
        part[k, :, 3 * mid :] = dot(cot_all[k], act2_all[...]).astype(BF16)
    part_copies += send_parts(pl.ds(3 * mid, mid))

    mean = reduce_end(red)
    scale1 = gain_in * rs1

    def last(at, _):
        grad_ref[at, :] = (
            cot_ref[at, :].astype(F32)
            + scale1 * (dact1[at, :] - mean[0:1] - h1[at, :] * mean[1:2])
        ).astype(BF16)

    each(rows, 16, last)()
    stores[1].start()

    for c in part_copies:
        c.wait_recv()
    total = parts[0].astype(F32)
    for k in range(1, group):
        total = total + parts[k].astype(F32)
    convg_ref[...] = total[:block, : 3 * mid]
    projg_ref[...] = total[:block, 3 * mid :]
    stores[2].start()
    stores[3].start()
    for c in stores:
        c.wait()

    for c in pending:
        c.wait_send()

    @pl.when(has_next)
    def _():
        up.wait_send()

    @pl.when(has_prev)
    def _():
        down.wait_send()


def copy_kernel(count, *refs):
    for i in range(count):
        refs[count + i][...] = refs[i][...]


def per_device(inputs, cotangent, conv_weight, proj_weight, gain_in, bias_in, gain_mid, bias_mid):
    samples, places, width = inputs.shape
    mid = proj_weight.shape[0]
    plan = Plan(
        lax.axis_size("seq"), lax.axis_size("dp"), samples, places, width, mid
    )
    rows, nz, nx, padded = plan.rows, plan.nz, plan.nx, plan.padded
    depth = nz * 2 * rows
    hbm = pl.BlockSpec(memory_space=pl.ANY)
    vmem = pl.BlockSpec(memory_space=pltpu.VMEM)
    outs = (
        jax.ShapeDtypeStruct((rows, width), BF16),
        jax.ShapeDtypeStruct((rows, width), BF16),
        jax.ShapeDtypeStruct((plan.block, 3 * mid), F32),
        jax.ShapeDtypeStruct((plan.block, mid), F32),
    )
    phases = len(plan.phases)
    results = pl.pallas_call(
        functools.partial(kernel, plan),
        out_shape=outs,
        in_specs=[hbm] * 8,
        out_specs=(hbm,) * 4,
        scratch_shapes=[
            pltpu.VMEM((rows, width), BF16),
            pltpu.VMEM((rows, width), BF16),
            pltpu.VMEM((width, 3 * mid), BF16),
            pltpu.VMEM((mid, width), BF16),
            pltpu.VMEM((width,), F32),
            pltpu.VMEM((width,), F32),
            pltpu.VMEM((mid,), F32),
            pltpu.VMEM((mid,), F32),
            *[pltpu.VMEM(o.shape, o.dtype) for o in outs],
            pltpu.VMEM((2, phases, 2, width), F32),
            pltpu.VMEM((2, phases, 2, mid), F32),
            pltpu.VMEM((2, plan.slots, 2, width), F32),
            pltpu.VMEM((2, plan.slots, 2, mid), F32),
            pltpu.VMEM((rows, width), BF16),
            pltpu.VMEM((rows, width), F32),
            pltpu.VMEM((rows, width), F32),
            pltpu.VMEM((rows, width), F32),
            pltpu.VMEM((rows, mid), F32),
            pltpu.VMEM((rows + EXTRA, mid), BF16),
            pltpu.VMEM((rows + EXTRA, mid), BF16),
            pltpu.VMEM((2, rows + EXTRA, mid), BF16),
            pltpu.VMEM((rows, width), F32),
            pltpu.VMEM((nz, nx, 2, padded, rows), BF16),
            pltpu.VMEM((nz, nx, 2, padded, rows), BF16),
            pltpu.VMEM((nx, padded, depth), BF16),
            pltpu.VMEM((nx, padded, depth), BF16),
            pltpu.VMEM((depth, mid), BF16),
            pltpu.VMEM((depth, mid), BF16),
            pltpu.VMEM((depth, mid), BF16),
            pltpu.VMEM((nz * 2 * (rows + EXTRA), mid), BF16),
            pltpu.VMEM((nx, padded, 4 * mid), BF16),
            pltpu.VMEM((nx * plan.m, padded, 4 * mid), BF16),
            pltpu.VMEM((nx * padded, 3 * mid), F32),
            pltpu.VMEM((rows, 3 * mid), BF16),
            pltpu.VMEM((2, 2 * rows, mid), F32),
            pltpu.SemaphoreType.DMA((plan.sems,)),
            pltpu.SemaphoreType.DMA((plan.sems,)),
            pltpu.SemaphoreType.DMA((14,)),
        ],
        compiler_params=pltpu.CompilerParams(
            collective_id=0, has_side_effects=True, vmem_limit_bytes=56 * 1024 * 1024
        ),
    )(
        inputs.reshape(rows, width),
        cotangent.reshape(rows, width),
        conv_weight,
        proj_weight,
        gain_in,
        bias_in,
        gain_mid,
        bias_mid,
    )
    block_out, input_grad, conv_grad, proj_grad = pl.pallas_call(
        functools.partial(copy_kernel, len(outs)),
        out_shape=outs,
        in_specs=[vmem] * len(outs),
        out_specs=(vmem,) * len(outs),
        compiler_params=pltpu.CompilerParams(vmem_limit_bytes=56 * 1024 * 1024),
    )(*results)
    shape = (samples, places, width)
    return (block_out.reshape(shape), input_grad.reshape(shape), conv_grad, proj_grad)


def solution(mesh):
    in_specs = (P("dp", "seq", None), P("dp", "seq", None), P(), P(), P(), P(), P(), P())
    out_specs = (P("dp", "seq", None), P("dp", "seq", None), P("seq", None), P("seq", None))
    return jax.shard_map(
        per_device, mesh=mesh, in_specs=in_specs, out_specs=out_specs, check_vma=False
    )
```
